128 devices in a mesh: gx: 16 (over z, x), gy: 8 (over y, core).
Axes of the slice: x: 4, y: 4, z: 4, core: 2. Of those that a mesh axis runs over, the one named last changes fastest.
Arguments:
- volume: bfloat16 [512, 512, 2, 512], P('gx', 'gy'), may hold values from -6 to 6
- spectra: bfloat16 [128, 512, 2, 128], P(('gx', 'gy')), may hold values from -6 to 6
- weights: float32 [128, 512, 2], P(('gx', 'gy')), may hold values from 0.1 to 1
- owners: int32 [128, 512, 2], P(('gx', 'gy')), may hold values from 0 to 127, all different within a row; in each aligned block of 512 rows (0 to 511, 512 to 1023, ..., all dimensions but the last counted through in order) at most 20 rows name the same one
- block_ids: int32 [128, 512, 2], P(('gx', 'gy')), may hold values from 0 to 8191
- pose_ids: int32 [128], P(('gx', 'gy')), may hold values from 0 to 63
- class_ids: int32 [128], P(('gx', 'gy')), may hold values from 0 to 15
- pose_shift: float32 [64, 2], replicated, may hold values from -4 to 4
- defocus: float32 [16], replicated, may hold values from 20 to 200
Outputs:
- real_map: bfloat16 [512, 512, 2, 512], P(None, 'gx', None, 'gy')
- update: float32 [512, 512, 2, 512], P('gx', 'gy')
- misfit: float32 [128], P(('gx', 'gy'))
The draws below stay inside these ranges and needn't reach their ends.
Inputs may be any that keep to these rules, and one draw needn't show every extreme that they name: Within the rows (particle, tile) of one device, each owner is named by at most 20 rows, and by exactly 20 rows in some device's rows; a row names two different owners.
All inputs are finite; a program needn't handle non-finite values.
Results may differ from the reference program's by a relative error of at most 0.008.
Values may be sent and summed in bfloat16 or wider, within the bound.
No kernel may reach another device: no remote copies, remote signals or barrier semaphores. Data moves between devices by JAX's collectives and lax.ppermute only.
A program may use at most 128 MiB of HBM per device.

```python
import math
import jax
import jax.numpy as jnp
import numpy as np
from jax import lax

L = 512
BLK = 128
BOX = 256
P_DEV = 1
NPOSE = 64
NCLASS = 16
PARTICLES = 128
TILES = 512
BLOCKS_DEV = 8192
CAP = 20
N_GX = 16
N_GY = 8
DEVICES = 128


def plant(drawn, stream_key, smallest, largest):
    index_at = [jax.random.randint(jax.random.fold_in(stream_key, axis), (), 0, length) for axis, length in enumerate(drawn.shape)]
    main_axis = drawn.shape.index(max(drawn.shape))
    beside = index_at[:main_axis] + [(index_at[main_axis] + 1) % drawn.shape[main_axis]] + index_at[main_axis + 1:]
    return drawn.at[tuple(index_at)].set(smallest).at[tuple(beside)].set(largest)


def block_levels(stream_key, extent, split, smallest, top_value):
    gain = 1.0
    for axis_at, parts in split:
        steps = jax.random.uniform(jax.random.fold_in(jax.random.fold_in(stream_key, 6), axis_at), (parts,), jnp.float32, smallest / len(split), top_value / len(split))
        gain = gain * jnp.repeat(jnp.exp(steps), extent[axis_at] // parts).reshape((-1,) + (1,) * (len(extent) - 1 - axis_at))
    return gain


def deal_out(rng, own, number, rows, count, top, most, lean):
    sequence = jax.random.permutation(rng, count)
    packed, usual = portions_of(count, rows * top, most, lean, True), portions_of(count, rows * top, most, lean, False)
    places = jnp.arange(count)

    def named(lengths, turn):
        used = int((lengths > 0).sum())
        fixed = max(1, used // 4)
        passed = fixed + (places - fixed + turn * (used - fixed)) % max(1, count - fixed)
        return jnp.zeros((count,), jnp.int32).at[sequence[jnp.where(places < fixed, places, passed)]].set(jnp.asarray(lengths, jnp.int32))

    lengths = jnp.where(number % 4 == 0, named(packed, number // 4), named(usual, number - number // 4 - 1))
    mixed = jax.random.permutation(jax.random.fold_in(own, 3), count)
    donor, taker = mixed[0:count // 2 * 2:2], mixed[1:count // 2 * 2:2]
    room = jnp.minimum(lengths[donor] - 1, most - lengths[taker]) // 2
    room = jnp.where((donor == sequence[0]) | (taker == sequence[0]) | (lengths[taker] == 0), 0, jnp.maximum(room, 0))
    passed = jax.random.randint(jax.random.fold_in(own, 4), (count // 2,), 0, 1 << 20) % (room + 1)
    lengths = lengths.at[donor].add(-passed).at[taker].add(passed)
    items = jnp.searchsorted(jnp.cumsum(lengths), jnp.arange(rows * top), side="right").astype(jnp.int32)
    grid = items.reshape(top, rows).T
    grid = grid[jax.random.permutation(jax.random.fold_in(own, 1), rows)]
    turn = jax.random.randint(jax.random.fold_in(own, 2), (rows, 1), 0, top)
    return jnp.take_along_axis(grid, (jnp.arange(top)[None, :] + turn) % top, axis=1)


def portions_of(number_of, total, bound, lean, full):
    loads = [(1 << 20) // math.isqrt(standing ** lean) + 1 for standing in range(1, number_of + 1)]
    largest = bound if full else min(bound, max(-(-total // number_of), total * loads[0] // sum(loads)))
    least = 1 if total - largest >= number_of - 1 else 0
    given, surplus = [largest] + [least] * (number_of - 1), total - largest - least * (number_of - 1)
    while surplus > 0:
        movable = [i for i in range(1, number_of) if given[i] < largest] or [i for i in range(1, number_of) if given[i] < bound]
        pool, left = sum([loads[i] for i in movable]), surplus
        for i in movable:
            extra = min(bound - given[i], max(1, left * loads[i] // pool), surplus)
            given[i] = given[i] + extra
            surplus = surplus - extra
    return np.array(given)


def normal_values(key, shape, deviation, reach, split=(), kind=jnp.bfloat16):
    drawn = jax.random.normal(key, shape, jnp.float32) * deviation
    if len(split) > 0:
        drawn = block_levels(key, shape, split, -0.22, 0.18) * drawn
    return jnp.clip(drawn, min=-reach, max=reach).astype(kind)


def setup_inputs(seed: int = 0) -> dict:
    streams_of = jax.random.split(jax.random.key(seed), 10)
    volume = normal_values(streams_of[0], (L, L, 2, L), 1.0, 6.0, ((0, 16), (1, 8)))
    spectra = normal_values(streams_of[1], (PARTICLES, TILES, 2, BLK), 1.0, 6.0, ((0, 128),))
    weights = jnp.clip(0.1 + 0.9 * jax.random.uniform(streams_of[2], (PARTICLES, TILES, 2), jnp.float32) ** block_levels(streams_of[2], (PARTICLES, TILES, 2), ((0, 128),), -0.2, 0.2), 0.1, 1.0)
    owners_keys = jax.random.split(jax.random.fold_in(streams_of[3], 1), PARTICLES * TILES // (P_DEV * TILES))
    owners_turns = jax.random.permutation(jax.random.fold_in(streams_of[3], 3), PARTICLES * TILES // (P_DEV * TILES))
    owners = jax.vmap(lambda own, number: deal_out(jax.random.fold_in(streams_of[3], 2), own, number, P_DEV * TILES, DEVICES, 2, CAP, 1))(owners_keys, owners_turns).reshape((PARTICLES, TILES, 2))
    block_ids = plant(jax.random.randint(streams_of[4], (PARTICLES, TILES, 2), 0, BLOCKS_DEV), jax.random.fold_in(streams_of[4], 1), 0, BLOCKS_DEV - 1).astype(jnp.int32)
    pose_ids = plant(jax.random.randint(streams_of[5], (PARTICLES,), 0, NPOSE), jax.random.fold_in(streams_of[5], 1), 0, NPOSE - 1).astype(jnp.int32)
    class_ids = plant(jax.random.randint(streams_of[6], (PARTICLES,), 0, NCLASS), jax.random.fold_in(streams_of[6], 1), 0, NCLASS - 1).astype(jnp.int32)
    pose_shift = jnp.clip(jax.random.uniform(streams_of[7], (NPOSE, 2), jnp.float32, -4.0, 4.0), -4.0, 4.0)
    defocus = jnp.clip(jnp.exp(jax.random.uniform(streams_of[8], (NCLASS,), jnp.float32, math.log(20.0), math.log(200.0))), 20.0, 200.0)
    return {"volume": volume, "spectra": spectra, "weights": weights, "owners": owners, "block_ids": block_ids, "pose_ids": pose_ids, "class_ids": class_ids, "pose_shift": pose_shift, "defocus": defocus}


def dft_matrix(length):
    indices = jnp.arange(length, dtype=jnp.int32)
    angles = (indices[:, None] * indices[None, :] % length).astype(jnp.float32) * (2.0 * math.pi / length)
    norm_factor = 1.0 / math.sqrt(length)
    cosine = jnp.cos(angles) * norm_factor
    sine_part = jnp.sin(angles) * norm_factor
    upper_rows = jnp.concatenate([cosine, sine_part], axis=1)
    lower_rows = jnp.concatenate([-sine_part, cosine], axis=1)
    return jnp.concatenate([upper_rows, lower_rows], axis=0).astype(jnp.bfloat16)

def frequencies(tile_count, block_len):
    pixel = jnp.arange(tile_count * block_len, dtype=jnp.int32).reshape(tile_count, block_len)
    freq_x = pixel % BOX
    freq_y = pixel // BOX
    freq_x = jnp.where(freq_x >= BOX // 2, freq_x - BOX, freq_x).astype(jnp.float32)
    freq_y = jnp.where(freq_y >= BOX // 2, freq_y - BOX, freq_y).astype(jnp.float32)
    radius_sq = (freq_x * freq_x + freq_y * freq_y) / (BOX * BOX / 4.0)
    return (freq_x, freq_y, radius_sq)

def particle_terms(spectrum, fetched, weights, shift_xy, defocus_part, geometry):
    freq_x, freq_y, radius_sq = geometry
    phase = -2.0 * math.pi / BOX * (freq_x[None] * shift_xy[:, 0, None, None] + freq_y[None] * shift_xy[:, 1, None, None])
    cosine = jnp.cos(phase)
    sine_part = jnp.sin(phase)
    spec_re = spectrum[:, :, 0, :]
    spec_im = spectrum[:, :, 1, :]
    shifted = jnp.stack([spec_re * cosine - spec_im * sine_part, spec_re * sine_part + spec_im * cosine], axis=2)
    ctf_value = -jnp.sin(defocus_part[:, None, None] * radius_sq[None] + 0.1)
    projected = weights[:, :, 0, None, None] * fetched[:, :, 0] + weights[:, :, 1, None, None] * fetched[:, :, 1]
    residual = shifted - ctf_value[:, :, None, :] * projected
    contribution = (weights[:, :, :, None, None] * ctf_value[:, :, None, None, :] * residual[:, :, None, :, :]).astype(jnp.bfloat16)
    misfit = lax.optimization_barrier(jnp.sum(residual * residual, axis=(1, 2, 3))) / (2.0 * spectrum.shape[1] * spectrum.shape[3])
    return (contribution, misfit)

def reference(volume, spectra, weights, owners, block_ids, pose_ids, class_ids, pose_shift, defocus):
    highest = lax.Precision.HIGHEST
    local_a = L // N_GX
    local_b = L // N_GY
    per_line = L // BLK
    block_rows = volume.reshape(N_GX, local_a, N_GY, local_b, 2, per_line, BLK).transpose(0, 2, 1, 3, 5, 4, 6).reshape(N_GX * N_GY * local_a * local_b * per_line, 2 * BLK)
    geometry = frequencies(TILES, BLK)
    global_ids = owners * BLOCKS_DEV + block_ids
    shift_xy = pose_shift[pose_ids]
    defocus_part = defocus[class_ids]
    groups = PARTICLES // P_DEV

    def per_group(group_items):
        spectrum_group, weight_group, id_group, shift_group, focus_group = group_items
        fetched = block_rows[id_group.reshape(-1)].astype(jnp.float32).reshape(P_DEV, TILES, 2, 2, BLK)
        return particle_terms(spectrum_group.astype(jnp.float32), fetched, weight_group, shift_group, focus_group, geometry)
    contribution, misfit = lax.map(per_group, (spectra.reshape(groups, P_DEV, TILES, 2, BLK), weights.reshape(groups, P_DEV, TILES, 2), global_ids.reshape(groups, P_DEV, TILES, 2), shift_xy.reshape(groups, P_DEV, 2), defocus_part.reshape(groups, P_DEV)))
    block_sums = jax.ops.segment_sum(contribution.reshape(-1, 2 * BLK).astype(jnp.float32), global_ids.reshape(-1), num_segments=N_GX * N_GY * BLOCKS_DEV)
    update = block_sums.reshape(N_GX, N_GY, local_a, local_b, per_line, 2, BLK).transpose(0, 2, 1, 3, 5, 4, 6).reshape(L, L, 2, L)
    inserted = (volume.astype(jnp.float32) + update).astype(jnp.bfloat16)
    matrix = dft_matrix(L).astype(jnp.float32)
    pass_c = jnp.dot(inserted.astype(jnp.float32).reshape(L * L, 2 * L), matrix, precision=highest).astype(jnp.bfloat16).reshape(L, L, 2, L)
    table_four = matrix.reshape(2, L, 2, L)
    pass_b = jnp.einsum('anrc,rnsk->aksc', pass_c.astype(jnp.float32), table_four, precision=highest).astype(jnp.bfloat16)
    real_map = jnp.einsum('nbrc,rnsk->kbsc', pass_b.astype(jnp.float32), table_four, precision=highest).astype(jnp.bfloat16)
    return (real_map, update, misfit.reshape(PARTICLES))
```

```python
import math

import jax
import jax.numpy as jnp
import numpy as np
from jax import lax
from jax.experimental import pallas as pl
from jax.experimental.pallas import tpu as pltpu
from jax.sharding import PartitionSpec as P

BOX = 256
CAP = 20
CHUNKS = 2
BF = jnp.bfloat16
F32 = jnp.float32
I32 = jnp.int32
VMEM_BYTES = 56 * 1024 * 1024


def dft_tables(length, gx, gy):
    n = np.arange(length)
    angles = (n[:, None] * n[None, :] % length) * (2.0 * np.pi / length)
    cosine = (np.cos(angles) / math.sqrt(length)).astype(BF)
    sine = (np.sin(angles) / math.sqrt(length)).astype(BF)
    upper = np.concatenate([cosine, sine], axis=1)
    lower = np.concatenate([-sine, cosine], axis=1)
    full = np.concatenate([upper, lower], axis=0)
    third = (
        full.reshape(2 * length, 2, gy, length // gy)
        .transpose(0, 2, 1, 3)
        .reshape(2 * length, 2 * length)
    )
    second = np.concatenate([cosine, sine], axis=1)
    local_a = length // gx
    rows = (
        np.arange(length).reshape(gx, CHUNKS, local_a // CHUNKS).transpose(1, 0, 2).reshape(length)
    )
    first = np.concatenate([cosine[rows], sine[rows]], axis=0)
    return third, second, first


def frequencies(tile_count, block_len):
    pixel = jnp.arange(tile_count * block_len, dtype=I32).reshape(tile_count, block_len)
    freq_x = pixel % BOX
    freq_y = pixel // BOX
    freq_x = jnp.where(freq_x >= BOX // 2, freq_x - BOX, freq_x).astype(F32)
    freq_y = jnp.where(freq_y >= BOX // 2, freq_y - BOX, freq_y).astype(F32)
    radius_sq = (freq_x * freq_x + freq_y * freq_y) / (BOX * BOX / 4.0)
    return (freq_x, freq_y, radius_sq)


def params(**more):
    return pltpu.CompilerParams(vmem_limit_bytes=VMEM_BYTES, **more)


def iota(shape, dim):
    return lax.broadcasted_iota(I32, shape, dim)


def dot(a, b):
    return jnp.dot(a, b, preferred_element_type=F32)


def shifted_index(iy, k, gy, direction):
    chips = gy // 2
    return ((iy // 2 + chips + direction * (k // 2)) % chips) * 2 + (iy % 2 + k % 2) % 2


def slots_kernel(own_ref, bid_ref, sent_ref, row_ref, col_ref):
    peers = sent_ref.shape[0]
    own = jnp.concatenate([own_ref[0:1, :], own_ref[1:2, :]], axis=1)
    bid = jnp.concatenate([bid_ref[0:1, :], bid_ref[1:2, :]], axis=1)
    count = own.shape[1]
    match = iota((peers, count), 0) == own
    hot = jnp.where(match, 1.0, 0.0).astype(F32)
    before = jnp.where(iota((count, count), 0) < iota((count, count), 1), 1.0, 0.0).astype(BF)
    prefix = dot(hot.astype(BF), before)
    slot = jnp.sum(hot * prefix, axis=0, keepdims=True)
    slot_i = slot.astype(I32)
    here = iota((peers, count), 0) == slot_i
    high = jnp.where(here, ((bid >> 6) + 1).astype(F32), 0.0).astype(BF)
    low = jnp.where(here, (bid & 63).astype(F32), 0.0).astype(BF)
    nt = (((1,), (1,)), ((), ()))
    hot_b = hot.astype(BF)
    high_at = lax.dot_general(hot_b, high, nt, preferred_element_type=F32)
    low_at = lax.dot_general(hot_b, low, nt, preferred_element_type=F32)
    sent_ref[...] = (high_at * 64.0 + low_at - 64.0).astype(I32)
    target = own * CAP + slot_i
    row_ref[...] = target
    wide = jnp.broadcast_to(target.astype(F32), (peers, count))
    col_ref[...] = wide.T.astype(I32)


def lookup_kernel(ids_ref, vol_ref, out_ref, tmp_ref):
    peers = ids_ref.shape[0]
    lines, width = vol_ref.shape
    half = width // 2
    group = 5
    for g in range(CAP // group):
        ids = jnp.concatenate(
            [jnp.broadcast_to(ids_ref[:, g * group + j : g * group + j + 1], (peers, 128)) for j in range(group)],
            axis=0,
        )
        line = ids >> 2
        part = ids & 3
        lanes = iota((group * peers, 128), 1)
        pick = jnp.concatenate(
            [jnp.where(line == lanes + 128 * b, 1.0, 0.0).astype(BF) for b in range(lines // 128)],
            axis=1,
        )
        found = dot(pick, vol_ref[...])
        for r in range(2):
            value = found[:, r * half : r * half + 128]
            for m in range(1, 4):
                value = jnp.where(part == m, found[:, r * half + m * 128 : r * half + (m + 1) * 128], value)
            for j in range(group):
                at = pl.ds(2 * (g * group + j) + r, peers, stride=2 * CAP)
                tmp_ref[at, :] = value[j * peers : (j + 1) * peers]
    out_ref[...] = tmp_ref[...].astype(BF)


def split_parts(rows_ref, tmp_ref):
    tmp_ref[...] = rows_ref[...].astype(F32)
    count = tmp_ref.shape[0] // 2
    return tmp_ref[pl.ds(0, count, stride=2), :], tmp_ref[pl.ds(1, count, stride=2), :]


def particle_kernel(ret_ref, col_ref, row_ref, w_ref, shift_ref, ctf_ref, out_ref, mis_ref, tmp_ref):
    total = ret_ref.shape[0] // 2
    tiles = w_ref.shape[0]
    lanes = iota((2 * tiles, 128), 1)
    col = col_ref[...]
    real, imag = split_parts(ret_ref, tmp_ref)
    blocks = jnp.concatenate([real, imag], axis=1).astype(BF)
    pick = jnp.concatenate(
        [jnp.where(col == lanes + 128 * b, 1.0, 0.0).astype(BF) for b in range(total // 128)], axis=1
    )
    fetched = dot(pick, blocks)
    w0 = w_ref[:, 0:1]
    w1 = w_ref[:, 1:2]
    projected = w0 * fetched[:tiles] + w1 * fetched[tiles:]
    ctf = ctf_ref[...]
    ctf2 = jnp.concatenate([ctf, ctf], axis=1)
    residual = shift_ref[...] - ctf2 * projected
    mis_ref[...] = jnp.sum(residual * residual, axis=0, keepdims=True)
    both = jnp.concatenate(
        [((w0 * ctf2) * residual).astype(BF), ((w1 * ctf2) * residual).astype(BF)], axis=0
    )
    row = row_ref[...]
    step = 512
    for b in range(total // step):
        put = jnp.where(iota((step, 2 * tiles), 0) + step * b == row, 1.0, 0.0).astype(BF)
        result = dot(put, both)
        for r in range(2):
            tmp_ref[pl.ds(2 * b * step + r, step, stride=2), :] = result[:, r * 128 : (r + 1) * 128]
    out_ref[...] = tmp_ref[...].astype(BF)


def insert_lines(first_line, inc_ref, line_ref, part_ref, vol_ref, table_ref, upd_ref, tmp_ref, exp_ref):
    total = exp_ref.shape[0]
    lines = vol_ref.shape[0]

    @pl.when(pl.program_id(0) == 0)
    def _():
        part = part_ref[...]
        for r, inc in enumerate(split_parts(inc_ref, tmp_ref)):
            for m in range(4):
                exp_ref[:, (r * 4 + m) * 128 : (r * 4 + m + 1) * 128] = jnp.where(part == m, inc, 0.0).astype(BF)

    base = first_line + pl.program_id(0) * lines
    pick = jnp.where(iota((lines, total), 0) + base == line_ref[...], 1.0, 0.0).astype(BF)
    update = dot(pick, exp_ref[...])
    upd_ref[...] = update
    inserted = (vol_ref[...].astype(F32) + update).astype(BF)
    return dot(inserted, table_ref[...])


def insert_first(inc_ref, line_ref, part_ref, vol_ref, table_ref, upd_ref, out_ref, tmp_ref, exp_ref):
    passed = insert_lines(0, inc_ref, line_ref, part_ref, vol_ref, table_ref, upd_ref, tmp_ref, exp_ref)
    for d in range(out_ref.shape[0]):
        out_ref[d] = passed[:, d * 128 : (d + 1) * 128].astype(BF)


def insert_next(first_line, iy_ref, inc_ref, line_ref, part_ref, vol_ref, table_ref, old_ref, upd_ref, *refs):
    outs = refs[:-3]
    tmp_ref, exp_ref, pass_ref = refs[-3:]
    passed = insert_lines(first_line, inc_ref, line_ref, part_ref, vol_ref, table_ref, upd_ref, tmp_ref, exp_ref)
    pass_ref[...] = passed.astype(BF)
    for k, out_ref in enumerate(outs):
        dest = shifted_index(iy_ref[0], k, len(outs), 1)
        out_ref[...] = pass_ref[:, pl.ds(pl.multiple_of(dest * 128, 128), 128)]


def second_lines(x, a, count, table_ref, tmp_ref):
    length, lanes = x.shape[0], x.shape[1] // 2
    sign = jnp.where(iota((1, 2 * lanes), 1) % lanes < lanes // 2, -1.0, 1.0).astype(F32)
    t0 = pltpu.roll(x[:, :lanes].astype(F32), lanes // 2, 1)
    t1 = pltpu.roll(x[:, lanes:].astype(F32), lanes // 2, 1)
    turned = (jnp.concatenate([t0, t1], axis=1) * sign).astype(BF)
    y = dot(table_ref[...], jnp.concatenate([x, turned], axis=0))
    tmp_ref[pl.ds(a, length, stride=count), :] = y[:, :lanes]
    tmp_ref[pl.ds(a + 1, length, stride=count), :] = y[:, lanes:]


def second_first(in_ref, table_ref, out_ref, tmp_ref):
    peers, count, rows, lanes = in_ref.shape
    length = peers * rows
    for a in range(0, count, 2):
        x = jnp.concatenate([in_ref[:, a + i].reshape(length, lanes) for i in range(2)], axis=1)
        second_lines(x, a, count, table_ref, tmp_ref)
    out_ref[...] = tmp_ref[...].astype(BF)


def second_next(iy_ref, *refs):
    ins = refs[:-4]
    table_ref, out_ref, tmp_ref, x_ref = refs[-4:]
    count, rows, lanes = ins[0].shape
    for a in range(0, count, 2):
        for k, ref in enumerate(ins):
            source = shifted_index(iy_ref[0], k, len(ins), -1)
            at = pl.ds(pl.multiple_of(source * rows, rows), rows)
            for i in range(2):
                x_ref[a // 2, at, i * lanes : (i + 1) * lanes] = ref[a + i]
    for a in range(0, count, 2):
        second_lines(x_ref[a // 2], a, count, table_ref, tmp_ref)
    out_ref[...] = tmp_ref[...].astype(BF)


def turn_rows(ref, b):
    x = ref[:, b]
    return x.reshape(x.shape[0] * x.shape[1], x.shape[2]).astype(F32).T


def turn_kernel(in_ref, out_ref):
    for b in range(in_ref.shape[1]):
        out_ref[b] = turn_rows(in_ref, b).astype(BF)


def first_kernel(early_ref, late_ref, table_ref, out_ref):
    group = out_ref.shape[0]
    half = out_ref.shape[2]
    rows = []
    for b in range(group):
        early = early_ref[b]
        late = turn_rows(late_ref, b).astype(BF)
        x = jnp.concatenate([early, late], axis=1)
        rows.append(jnp.concatenate([x, jnp.concatenate([-x[half:], x[:half]], axis=0)], axis=1))
    y = dot(jnp.concatenate(rows, axis=0), table_ref[...])
    for b in range(group):
        for s in range(2):
            at = (2 * b + s) * half
            out_ref[b, s] = y[at : at + half].astype(BF)


def local(volume, spectra, weights, owners, block_ids, pose_ids, class_ids, pose_shift, defocus):
    gx = lax.axis_size("gx")
    gy = lax.axis_size("gy")
    peers = gx * gy
    local_a, local_b, _, length = volume.shape
    tiles = spectra.shape[1]
    block_len = spectra.shape[3]
    lines = local_a * local_b
    total = peers * CAP
    rows = 2 * total
    refs = 2 * tiles
    third, second, first = dft_tables(length, gx, gy)
    whole = pl.BlockSpec(memory_space=pltpu.VMEM)

    own = owners.transpose(0, 2, 1).reshape(2, tiles)
    bid = block_ids.transpose(0, 2, 1).reshape(2, tiles)
    sent, row, col = pl.pallas_call(
        slots_kernel,
        out_shape=(
            jax.ShapeDtypeStruct((peers, 128), I32),
            jax.ShapeDtypeStruct((1, refs), I32),
            jax.ShapeDtypeStruct((refs, 128), I32),
        ),
        in_specs=[whole] * 2,
        out_specs=(whole,) * 3,
        compiler_params=params(),
        name="slots",
    )(own, bid)
    got = lax.all_to_all(
        sent.reshape(peers, 1, 128), ("gx", "gy"), split_axis=0, concat_axis=0, tiled=True
    ).reshape(peers, 128)

    vol = volume.reshape(lines, 2 * length)
    looked = pl.pallas_call(
        lookup_kernel,
        out_shape=jax.ShapeDtypeStruct((rows, block_len), BF),
        in_specs=[whole] * 2,
        out_specs=whole,
        scratch_shapes=[pltpu.VMEM((rows, block_len), F32)],
        compiler_params=params(),
        name="lookup",
    )(got, vol)
    returned = lax.all_to_all(
        looked.reshape(peers, 2 * CAP, block_len), ("gx", "gy"), split_axis=0, concat_axis=0, tiled=True
    ).reshape(rows, block_len)

    class_match = class_ids[:, None] == jnp.arange(defocus.shape[0], dtype=I32)[None, :]
    defocus_part = jnp.sum(jnp.where(class_match, defocus[None, :], 0.0), axis=1)
    pose_match = pose_ids[:, None, None] == jnp.arange(pose_shift.shape[0], dtype=I32)[None, :, None]
    shift_xy = jnp.sum(jnp.where(pose_match, pose_shift[None, :, :], 0.0), axis=1)
    freq_x, freq_y, radius_sq = frequencies(tiles, block_len)
    phase = -2.0 * math.pi / BOX * (freq_x * shift_xy[0, 0] + freq_y * shift_xy[0, 1])
    cosine = jnp.cos(phase)
    sine = jnp.sin(phase)
    spec_re = spectra[0, :, 0, :].astype(F32)
    spec_im = spectra[0, :, 1, :].astype(F32)
    shifted = jnp.concatenate([spec_re * cosine - spec_im * sine, spec_re * sine + spec_im * cosine], axis=1)
    ctf = -jnp.sin(defocus_part[0] * radius_sq + 0.1)

    ids = got[:, :CAP].reshape(total)
    line_row = (ids >> 2).reshape(1, total)
    part_col = jnp.broadcast_to((ids & 3)[:, None], (total, 128))
    weight = weights.reshape(tiles, 2)
    returned, line_row, part_col, weight, shifted, ctf = lax.optimization_barrier(
        (returned, line_row, part_col, weight, shifted, ctf)
    )

    outgoing, squares = pl.pallas_call(
        particle_kernel,
        out_shape=(
            jax.ShapeDtypeStruct((rows, block_len), BF),
            jax.ShapeDtypeStruct((1, 2 * block_len), F32),
        ),
        in_specs=[whole] * 6,
        out_specs=(whole,) * 2,
        scratch_shapes=[pltpu.VMEM((rows, block_len), F32)],
        compiler_params=params(),
        name="particle",
    )(returned, col, row, weight, shifted, ctf)
    incoming = lax.all_to_all(
        outgoing.reshape(peers, 2 * CAP, block_len), ("gx", "gy"), split_axis=0, concat_axis=0, tiled=True
    ).reshape(rows, block_len)
    misfit = (jnp.sum(squares) / (2.0 * tiles * block_len)).reshape(1)

    iy = lax.axis_index("gy").astype(I32).reshape(1)
    scalars = pl.BlockSpec(memory_space=pltpu.SMEM)

    chunk_a = local_a // CHUNKS
    chunk_lines = lines // CHUNKS
    step = 256
    steps = chunk_lines // step
    insert_scratch = [pltpu.VMEM((rows, block_len), F32), pltpu.VMEM((total, 2 * length), BF)]
    update, out0 = pl.pallas_call(
        insert_first,
        grid=(steps,),
        out_shape=(
            jax.ShapeDtypeStruct((lines, 2 * length), F32),
            jax.ShapeDtypeStruct((gy, chunk_lines, 128), BF),
        ),
        in_specs=[whole] * 3 + [pl.BlockSpec((step, 2 * length), lambda i: (i, 0)), whole],
        out_specs=(
            pl.BlockSpec((step, 2 * length), lambda i: (i, 0)),
            pl.BlockSpec((gy, step, 128), lambda i: (0, i, 0)),
        ),
        scratch_shapes=insert_scratch,
        compiler_params=params(dimension_semantics=("arbitrary",)),
        name="insert0",
    )(incoming, line_row, part_col, vol, third)
    along0 = lax.all_to_all(out0, "gy", split_axis=0, concat_axis=0, tiled=True)
    update, *pieces = pl.pallas_call(
        lambda *r: insert_next(chunk_lines, *r),
        grid=(steps,),
        out_shape=(jax.ShapeDtypeStruct((lines, 2 * length), F32),)
        + (jax.ShapeDtypeStruct((chunk_lines, 128), BF),) * gy,
        in_specs=[scalars]
        + [whole] * 3
        + [pl.BlockSpec((step, 2 * length), lambda i: (i + steps, 0)), whole, pl.BlockSpec(memory_space=pl.ANY)],
        out_specs=(pl.BlockSpec((step, 2 * length), lambda i: (i + steps, 0)),)
        + (pl.BlockSpec((step, 128), lambda i: (i, 0)),) * gy,
        scratch_shapes=insert_scratch + [pltpu.VMEM((step, 2 * length), BF)],
        input_output_aliases={6: 0},
        compiler_params=params(dimension_semantics=("arbitrary",)),
        name="insert1",
    )(iy, incoming, line_row, part_col, vol, third, update)
    along0, pieces = lax.optimization_barrier((along0, pieces))
    arrived = [pieces[0]]
    for k in range(1, gy):
        pairs = [(i, shifted_index(i, k, gy, 1)) for i in range(gy)]
        arrived.append(lax.ppermute(pieces[k], "gy", pairs))

    second_out = jax.ShapeDtypeStruct((length * chunk_a, 128), BF)
    second_tmp = pltpu.VMEM((length * chunk_a, 128), F32)
    lines0 = pl.pallas_call(
        second_first,
        out_shape=second_out,
        in_specs=[whole] * 2,
        out_specs=whole,
        scratch_shapes=[second_tmp],
        compiler_params=params(),
        name="second0",
    )(along0.reshape(gy, chunk_a, local_b, 128), second)

    def cross(x):
        x = x.reshape(gx, (length // gx) * chunk_a, 128)
        return lax.all_to_all(x, "gx", split_axis=0, concat_axis=0, tiled=True).reshape(
            gx, length // gx, chunk_a, 128
        )

    early = cross(lines0)
    lines1 = pl.pallas_call(
        second_next,
        out_shape=second_out,
        in_specs=[scalars] + [whole] * (gy + 1),
        out_specs=whole,
        scratch_shapes=[second_tmp, pltpu.VMEM((chunk_a // 2, length, 256), BF)],
        compiler_params=params(),
        name="second1",
    )(iy, *[x.reshape(chunk_a, local_b, 128) for x in arrived], second)
    late = cross(lines1)
    out_b = length // gx
    out_c = length // gy
    group = 4
    turned = pl.pallas_call(
        turn_kernel,
        grid=(out_b // group,),
        out_shape=jax.ShapeDtypeStruct((out_b, 128, gx * chunk_a), BF),
        in_specs=[pl.BlockSpec((gx, group, chunk_a, 128), lambda i: (0, i, 0, 0))],
        out_specs=pl.BlockSpec((group, 128, gx * chunk_a), lambda i: (i, 0, 0)),
        compiler_params=params(dimension_semantics=("arbitrary",)),
        name="turn",
    )(early)
    real_map = pl.pallas_call(
        first_kernel,
        grid=(out_b // group,),
        out_shape=jax.ShapeDtypeStruct((out_b, 2, out_c, length), BF),
        in_specs=[
            pl.BlockSpec((group, 128, gx * chunk_a), lambda i: (i, 0, 0)),
            pl.BlockSpec((gx, group, chunk_a, 128), lambda i: (0, i, 0, 0)),
            whole,
        ],
        out_specs=pl.BlockSpec((group, 2, out_c, length), lambda i: (i, 0, 0, 0)),
        compiler_params=params(dimension_semantics=("arbitrary",)),
        name="first",
    )(turned, late, first)
    update = update.reshape(local_a, local_b, 2, length)
    return (real_map.transpose(3, 0, 1, 2), update, misfit)


def solution(mesh):
    in_specs = (
        P("gx", "gy", None, None),
        P(("gx", "gy"), None, None, None),
        P(("gx", "gy"), None, None),
        P(("gx", "gy"), None, None),
        P(("gx", "gy"), None, None),
        P(("gx", "gy")),
        P(("gx", "gy")),
        P(),
        P(),
    )
    out_specs = (P(None, "gx", None, "gy"), P("gx", "gy", None, None), P(("gx", "gy")))
    return jax.shard_map(local, mesh=mesh, in_specs=in_specs, out_specs=out_specs, check_vma=False)
```

```python
import math

import jax
import jax.numpy as jnp
import numpy as np
from jax import lax
from jax.experimental import pallas as pl
from jax.experimental.pallas import tpu as pltpu
from jax.sharding import PartitionSpec as P

BOX = 256
CAP = 20
CHUNKS = (16, 16)
BF = jnp.bfloat16
F32 = jnp.float32
I32 = jnp.int32
VMEM_BYTES = 52 * 1024 * 1024


def dft_tables(length, gx, gy):
    n = np.arange(length)
    angles = (n[:, None] * n[None, :] % length) * (2.0 * np.pi / length)
    cosine = (np.cos(angles) / math.sqrt(length)).astype(BF)
    sine = (np.sin(angles) / math.sqrt(length)).astype(BF)
    upper = np.concatenate([cosine, sine], axis=1)
    lower = np.concatenate([-sine, cosine], axis=1)
    full = np.concatenate([upper, lower], axis=0)
    third = (
        full.reshape(2 * length, 2, gy, length // gy)
        .transpose(0, 2, 1, 3)
        .reshape(2 * length, 2 * length)
    )
    second = np.concatenate([cosine, sine], axis=1)
    local_a = length // gx
    lines = np.arange(length).reshape(gx, local_a)
    starts = np.cumsum((0,) + CHUNKS)
    rows = np.concatenate(
        [lines[:, starts[j] : starts[j + 1]].reshape(-1) for j in range(len(CHUNKS))]
    )
    first = np.concatenate([cosine[rows], sine[rows]], axis=0)
    return third, second, first


def frequencies(tile_count, block_len):
    pixel = jnp.arange(tile_count * block_len, dtype=I32).reshape(tile_count, block_len)
    freq_x = pixel % BOX
    freq_y = pixel // BOX
    freq_x = jnp.where(freq_x >= BOX // 2, freq_x - BOX, freq_x).astype(F32)
    freq_y = jnp.where(freq_y >= BOX // 2, freq_y - BOX, freq_y).astype(F32)
    radius_sq = (freq_x * freq_x + freq_y * freq_y) / (BOX * BOX / 4.0)
    return (freq_x, freq_y, radius_sq)


def params(**more):
    return pltpu.CompilerParams(vmem_limit_bytes=VMEM_BYTES, **more)


def near(x):
    return pltpu.with_memory_space_constraint(x, pltpu.VMEM)


def iota(shape, dim):
    return lax.broadcasted_iota(I32, shape, dim)


def dot(a, b):
    return jnp.dot(a, b, preferred_element_type=F32)


def shifted_index(iy, k, gy, direction):
    chips = gy // 2
    return ((iy // 2 + chips + direction * (k // 2)) % chips) * 2 + (iy % 2 + k % 2) % 2


def slots_kernel(own_ref, bid_ref, sent_ref, row_ref, col_ref):
    peers = sent_ref.shape[0]
    own = jnp.concatenate([own_ref[0:1, :], own_ref[1:2, :]], axis=1)
    bid = jnp.concatenate([bid_ref[0:1, :], bid_ref[1:2, :]], axis=1)
    count = own.shape[1]
    match = iota((peers, count), 0) == own
    hot = jnp.where(match, 1.0, 0.0).astype(F32)
    before = jnp.where(iota((count, count), 0) < iota((count, count), 1), 1.0, 0.0).astype(BF)
    prefix = dot(hot.astype(BF), before)
    slot = jnp.sum(hot * prefix, axis=0, keepdims=True)
    slot_i = slot.astype(I32)
    here = iota((peers, count), 0) == slot_i
    high = jnp.where(here, ((bid >> 6) + 1).astype(F32), 0.0).astype(BF)
    low = jnp.where(here, (bid & 63).astype(F32), 0.0).astype(BF)
    nt = (((1,), (1,)), ((), ()))
    hot_b = hot.astype(BF)
    high_at = lax.dot_general(hot_b, high, nt, preferred_element_type=F32)
    low_at = lax.dot_general(hot_b, low, nt, preferred_element_type=F32)
    sent_ref[...] = (high_at * 64.0 + low_at - 64.0).astype(I32)
    target = own * CAP + slot_i
    row_ref[...] = target
    wide = jnp.broadcast_to(target.astype(F32), (peers, count))
    col_ref[...] = wide.T.astype(I32)


def lookup_kernel(ids_ref, vol_ref, out_ref, tmp_ref):
    def peer(p, carry):
        at = pl.multiple_of(p * (2 * CAP), 8)
        for s in range(CAP):
            block = jnp.maximum(ids_ref[p, s], 0)
            tmp_ref[pl.ds(at + 2 * s, 2), :] = vol_ref[pl.ds(pl.multiple_of(2 * block, 2), 2), :]
        return carry

    lax.fori_loop(0, ids_ref.shape[0], peer, 0)
    out_ref[...] = tmp_ref[...].astype(BF)


def parts_kernel(part_ref, out_ref):
    wide = jnp.broadcast_to(part_ref[...].astype(F32), (out_ref.shape[1], out_ref.shape[0]))
    out_ref[...] = wide.T.astype(I32)


def split_parts(rows_ref, tmp_ref):
    tmp_ref[...] = rows_ref[...].astype(F32)
    count = tmp_ref.shape[0] // 2
    return tmp_ref[pl.ds(0, count, stride=2), :], tmp_ref[pl.ds(1, count, stride=2), :]


def particle_kernel(ret_ref, col_ref, row_ref, w_ref, shift_ref, ctf_ref, out_ref, mis_ref, tmp_ref):
    total = ret_ref.shape[0] // 2
    tiles = w_ref.shape[0]
    lanes = iota((2 * tiles, 128), 1)
    col = col_ref[...]
    real, imag = split_parts(ret_ref, tmp_ref)
    blocks = jnp.concatenate([real, imag], axis=1).astype(BF)
    pick = jnp.concatenate(
        [jnp.where(col == lanes + 128 * b, 1.0, 0.0).astype(BF) for b in range(total // 128)], axis=1
    )
    fetched = dot(pick, blocks)
    w0 = w_ref[:, 0:1]
    w1 = w_ref[:, 1:2]
    projected = w0 * fetched[:tiles] + w1 * fetched[tiles:]
    ctf = ctf_ref[...]
    ctf2 = jnp.concatenate([ctf, ctf], axis=1)
    residual = shift_ref[...] - ctf2 * projected
    mis_ref[...] = jnp.sum(residual * residual, axis=0, keepdims=True)
    both = jnp.concatenate(
        [((w0 * ctf2) * residual).astype(BF), ((w1 * ctf2) * residual).astype(BF)], axis=0
    )
    row = row_ref[...]
    step = 512
    for b in range(total // step):
        put = jnp.where(iota((step, 2 * tiles), 0) + step * b == row, 1.0, 0.0).astype(BF)
        result = dot(put, both)
        for r in range(2):
            tmp_ref[pl.ds(2 * b * step + r, step, stride=2), :] = result[:, r * 128 : (r + 1) * 128]
    out_ref[...] = tmp_ref[...].astype(BF)


def insert_lines(first_line, inc_ref, line_ref, part_ref, vol_ref, table_ref, upd_ref, tmp_ref, exp_ref):
    total = exp_ref.shape[0]
    lines = vol_ref.shape[0]

    @pl.when(pl.program_id(0) == 0)
    def _():
        part = part_ref[...]
        for r, inc in enumerate(split_parts(inc_ref, tmp_ref)):
            for m in range(4):
                exp_ref[:, (r * 4 + m) * 128 : (r * 4 + m + 1) * 128] = jnp.where(part == m, inc, 0.0).astype(BF)

    base = first_line + pl.program_id(0) * lines
    pick = jnp.where(iota((lines, total), 0) + base == line_ref[...], 1.0, 0.0).astype(BF)
    update = dot(pick, exp_ref[...])
    upd_ref[...] = update
    inserted = (vol_ref[...].astype(F32) + update).astype(BF)
    return dot(inserted, table_ref[...])


def insert_first(inc_ref, line_ref, part_ref, vol_ref, table_ref, upd_ref, out_ref, tmp_ref, exp_ref):
    passed = insert_lines(0, inc_ref, line_ref, part_ref, vol_ref, table_ref, upd_ref, tmp_ref, exp_ref)
    for d in range(out_ref.shape[0]):
        out_ref[d] = passed[:, d * 128 : (d + 1) * 128].astype(BF)


def insert_next(first_line, iy_ref, inc_ref, line_ref, part_ref, vol_ref, table_ref, old_ref, upd_ref, *refs):
    outs = refs[:-3]
    tmp_ref, exp_ref, pass_ref = refs[-3:]
    passed = insert_lines(first_line, inc_ref, line_ref, part_ref, vol_ref, table_ref, upd_ref, tmp_ref, exp_ref)
    pass_ref[...] = passed.astype(BF)
    for k, out_ref in enumerate(outs):
        dest = shifted_index(iy_ref[0], k, len(outs), 1)
        out_ref[...] = pass_ref[:, pl.ds(pl.multiple_of(dest * 128, 128), 128)]


def second_lines(x, a, count, table_ref, tmp_ref):
    length, lanes = x.shape[0], x.shape[1] // 2
    sign = jnp.where(iota((1, 2 * lanes), 1) % lanes < lanes // 2, -1.0, 1.0).astype(F32)
    t0 = pltpu.roll(x[:, :lanes].astype(F32), lanes // 2, 1)
    t1 = pltpu.roll(x[:, lanes:].astype(F32), lanes // 2, 1)
    turned = (jnp.concatenate([t0, t1], axis=1) * sign).astype(BF)
    y = dot(table_ref[...], jnp.concatenate([x, turned], axis=0))
    tmp_ref[pl.ds(a, length, stride=count), :] = y[:, :lanes]
    tmp_ref[pl.ds(a + 1, length, stride=count), :] = y[:, lanes:]


def second_first(in_ref, table_ref, out_ref, tmp_ref):
    peers, count, rows, lanes = in_ref.shape
    length = peers * rows
    for a in range(0, count, 2):
        x = jnp.concatenate([in_ref[:, a + i].reshape(length, lanes) for i in range(2)], axis=1)
        second_lines(x, a, count, table_ref, tmp_ref)
    out_ref[...] = tmp_ref[...].astype(BF)


def second_next(iy_ref, *refs):
    ins = refs[:-4]
    table_ref, out_ref, tmp_ref, x_ref = refs[-4:]
    count, rows, lanes = ins[0].shape
    for a in range(0, count, 2):
        for k, ref in enumerate(ins):
            source = shifted_index(iy_ref[0], k, len(ins), -1)
            at = pl.ds(pl.multiple_of(source * rows, rows), rows)
            for i in range(2):
                x_ref[a // 2, at, i * lanes : (i + 1) * lanes] = ref[a + i]
    for a in range(0, count, 2):
        second_lines(x_ref[a // 2], a, count, table_ref, tmp_ref)
    out_ref[...] = tmp_ref[...].astype(BF)


def turn_rows(ref, b):
    x = ref[:, b]
    return x.reshape(x.shape[0] * x.shape[1], x.shape[2]).astype(F32).T


def turn_kernel(in_ref, out_ref):
    for b in range(in_ref.shape[1]):
        out_ref[b] = turn_rows(in_ref, b).astype(BF)


def first_kernel(*refs):
    *early_refs, late_ref, table_ref, out_ref = refs
    group = out_ref.shape[0]
    half = out_ref.shape[2]
    rows = []
    for b in range(group):
        late = turn_rows(late_ref, b).astype(BF)
        x = jnp.concatenate([ref[b] for ref in early_refs] + [late], axis=1)
        rows.append(jnp.concatenate([x, jnp.concatenate([-x[half:], x[:half]], axis=0)], axis=1))
    y = dot(jnp.concatenate(rows, axis=0), table_ref[...])
    for b in range(group):
        for s in range(2):
            at = (2 * b + s) * half
            out_ref[b, s] = y[at : at + half].astype(BF)


def local(volume, spectra, weights, owners, block_ids, pose_ids, class_ids, pose_shift, defocus):
    gx = lax.axis_size("gx")
    gy = lax.axis_size("gy")
    peers = gx * gy
    local_a, local_b, _, length = volume.shape
    tiles = spectra.shape[1]
    block_len = spectra.shape[3]
    lines = local_a * local_b
    total = peers * CAP
    rows = 2 * total
    refs = 2 * tiles
    third, second, first = dft_tables(length, gx, gy)
    whole = pl.BlockSpec(memory_space=pltpu.VMEM)

    own = owners.transpose(0, 2, 1).reshape(2, tiles)
    bid = block_ids.transpose(0, 2, 1).reshape(2, tiles)
    sent, row, col = pl.pallas_call(
        slots_kernel,
        out_shape=(
            jax.ShapeDtypeStruct((peers, 128), I32),
            jax.ShapeDtypeStruct((1, refs), I32),
            jax.ShapeDtypeStruct((refs, 128), I32),
        ),
        in_specs=[whole] * 2,
        out_specs=(whole,) * 3,
        compiler_params=params(),
        name="slots",
    )(own, bid)
    got = lax.all_to_all(
        sent.reshape(peers, 1, 128), ("gx", "gy"), split_axis=0, concat_axis=0, tiled=True
    ).reshape(peers, 128)

    scalars = pl.BlockSpec(memory_space=pltpu.SMEM)
    vol = volume.reshape(lines, 2 * length)
    per_line = length // block_len
    vol_rows = (
        volume.astype(F32)
        .reshape(lines, 2, per_line, block_len)
        .transpose(0, 2, 1, 3)
        .reshape(lines * per_line * 2, block_len)
    )
    looked = pl.pallas_call(
        lookup_kernel,
        out_shape=jax.ShapeDtypeStruct((rows, block_len), BF),
        in_specs=[scalars, whole],
        out_specs=whole,
        scratch_shapes=[pltpu.VMEM((rows, block_len), F32)],
        compiler_params=params(),
        name="lookup",
    )(got, vol_rows)
    returned = lax.all_to_all(
        looked.reshape(peers, 2 * CAP, block_len), ("gx", "gy"), split_axis=0, concat_axis=0, tiled=True
    ).reshape(rows, block_len)

    class_match = class_ids[:, None] == jnp.arange(defocus.shape[0], dtype=I32)[None, :]
    defocus_part = jnp.sum(jnp.where(class_match, defocus[None, :], 0.0), axis=1)
    pose_match = pose_ids[:, None, None] == jnp.arange(pose_shift.shape[0], dtype=I32)[None, :, None]
    shift_xy = jnp.sum(jnp.where(pose_match, pose_shift[None, :, :], 0.0), axis=1)
    freq_x, freq_y, radius_sq = frequencies(tiles, block_len)
    phase = -2.0 * math.pi / BOX * (freq_x * shift_xy[0, 0] + freq_y * shift_xy[0, 1])
    cosine = jnp.cos(phase)
    sine = jnp.sin(phase)
    spec_re = spectra[0, :, 0, :].astype(F32)
    spec_im = spectra[0, :, 1, :].astype(F32)
    shifted = jnp.concatenate([spec_re * cosine - spec_im * sine, spec_re * sine + spec_im * cosine], axis=1)
    ctf = -jnp.sin(defocus_part[0] * radius_sq + 0.1)

    ids = jnp.maximum(got[:, :CAP].reshape(1, total), -4)
    line_row = ids >> 2
    part_row = ids & 3
    weight = weights.reshape(tiles, 2)
    returned, line_row, part_row, weight, shifted, ctf = lax.optimization_barrier(
        (returned, line_row, part_row, weight, shifted, ctf)
    )
    part_col = pl.pallas_call(
        parts_kernel,
        out_shape=jax.ShapeDtypeStruct((total, 128), I32),
        in_specs=[whole],
        out_specs=whole,
        compiler_params=params(),
        cost_estimate=pl.CostEstimate(flops=1 << 22, bytes_accessed=1 << 22, transcendentals=0),
        name="parts",
    )(part_row)

    outgoing, squares = pl.pallas_call(
        particle_kernel,
        out_shape=(
            jax.ShapeDtypeStruct((rows, block_len), BF),
            jax.ShapeDtypeStruct((1, 2 * block_len), F32),
        ),
        in_specs=[whole] * 6,
        out_specs=(whole,) * 2,
        scratch_shapes=[pltpu.VMEM((rows, block_len), F32)],
        compiler_params=params(),
        name="particle",
    )(near(returned), col, row, weight, shifted, ctf)
    incoming = lax.all_to_all(
        outgoing.reshape(peers, 2 * CAP, block_len), ("gx", "gy"), split_axis=0, concat_axis=0, tiled=True
    ).reshape(rows, block_len)
    misfit = (jnp.sum(squares) / (2.0 * tiles * block_len)).reshape(1)
    incoming, part_col = lax.optimization_barrier((incoming, part_col))

    iy = lax.axis_index("gy").astype(I32).reshape(1)
    step = 256
    insert_scratch = [pltpu.VMEM((rows, block_len), F32), pltpu.VMEM((total, 2 * length), BF)]
    update_shape = jax.ShapeDtypeStruct((lines, 2 * length), F32)

    def second_shapes(count):
        return {
            "out_shape": jax.ShapeDtypeStruct((length * count, 128), BF),
            "out_specs": whole,
            "compiler_params": params(),
        }

    def cross(x, count):
        x = x.reshape(gx, (length // gx) * count, 128)
        return lax.all_to_all(x, "gx", split_axis=0, concat_axis=0, tiled=True).reshape(
            gx, length // gx, count, 128
        )

    crossed = []
    before = None
    start = 0
    for j, count in enumerate(CHUNKS):
        chunk_lines = count * local_b
        steps = chunk_lines // step
        skip = start * local_b // step
        block = pl.BlockSpec((step, 2 * length), lambda i, skip=skip: (i + skip, 0))
        if j == 0:
            update, out = pl.pallas_call(
                insert_first,
                grid=(steps,),
                out_shape=(update_shape, jax.ShapeDtypeStruct((gy, chunk_lines, 128), BF)),
                in_specs=[whole] * 3 + [block, whole],
                out_specs=(block, pl.BlockSpec((gy, step, 128), lambda i: (0, i, 0))),
                scratch_shapes=insert_scratch,
                compiler_params=params(dimension_semantics=("arbitrary",)),
                name="insert0",
            )(near(incoming), line_row, near(part_col), vol, third)
            arrived = lax.all_to_all(out, "gy", split_axis=0, concat_axis=0, tiled=True)
        else:
            update, *pieces = pl.pallas_call(
                lambda *r, first_line=start * local_b: insert_next(first_line, *r),
                grid=(steps,),
                out_shape=(update_shape,) + (jax.ShapeDtypeStruct((chunk_lines, 128), BF),) * gy,
                in_specs=[scalars] + [whole] * 3 + [block, whole, pl.BlockSpec(memory_space=pl.ANY)],
                out_specs=(block,) + (pl.BlockSpec((step, 128), lambda i: (i, 0)),) * gy,
                scratch_shapes=insert_scratch + [pltpu.VMEM((step, 2 * length), BF)],
                input_output_aliases={6: 0},
                compiler_params=params(dimension_semantics=("arbitrary",)),
                name=f"insert{j}",
            )(iy, incoming, line_row, part_col, vol, third, update)
            before, pieces = lax.optimization_barrier((before, pieces))
            arrived = [pieces[0]]
            for k in range(1, gy):
                pairs = [(i, shifted_index(i, k, gy, 1)) for i in range(gy)]
                arrived.append(lax.ppermute(pieces[k], "gy", pairs))
        if before is not None:
            crossed.append((before, start - CHUNKS[j - 1], CHUNKS[j - 1]))
        before = arrived
        start += count
    crossed.append((before, start - CHUNKS[-1], CHUNKS[-1]))

    for j, (arrived, start, count) in enumerate(crossed):
        tmp = pltpu.VMEM((length * count, 128), F32)
        if j == 0:
            done = pl.pallas_call(
                second_first,
                in_specs=[whole] * 2,
                scratch_shapes=[tmp],
                name="second0",
                **second_shapes(count),
            )(near(arrived.reshape(gy, count, local_b, 128)), second)
        else:
            done = pl.pallas_call(
                second_next,
                in_specs=[scalars] + [whole] * (gy + 1),
                scratch_shapes=[tmp, pltpu.VMEM((count // 2, length, 256), BF)],
                name=f"second{j}",
                **second_shapes(count),
            )(iy, *[x.reshape(count, local_b, 128) for x in arrived], second)
        crossed[j] = cross(done, count)

    out_b = length // gx
    out_c = length // gy
    group = 8

    def rows_spec(count):
        return pl.BlockSpec((gx, group, count, 128), lambda i: (0, i, 0, 0))

    def turned_spec(count):
        return pl.BlockSpec((group, 128, gx * count), lambda i: (i, 0, 0))

    turned = [
        pl.pallas_call(
            turn_kernel,
            grid=(out_b // group,),
            out_shape=jax.ShapeDtypeStruct((out_b, 128, gx * count), BF),
            in_specs=[rows_spec(count)],
            out_specs=turned_spec(count),
            compiler_params=params(dimension_semantics=("arbitrary",)),
            name=f"turn{j}",
        )(crossed[j])
        for j, count in enumerate(CHUNKS[:-1])
    ]
    real_map = pl.pallas_call(
        first_kernel,
        grid=(out_b // group,),
        out_shape=jax.ShapeDtypeStruct((out_b, 2, out_c, length), BF),
        in_specs=[turned_spec(count) for count in CHUNKS[:-1]] + [rows_spec(CHUNKS[-1]), whole],
        out_specs=pl.BlockSpec((group, 2, out_c, length), lambda i: (i, 0, 0, 0)),
        compiler_params=params(dimension_semantics=("arbitrary",)),
        name="first",
    )(*turned, crossed[-1], first)
    update = update.reshape(local_a, local_b, 2, length)
    return (real_map.transpose(3, 0, 1, 2), update, misfit)


def solution(mesh):
    in_specs = (
        P("gx", "gy", None, None),
        P(("gx", "gy"), None, None, None),
        P(("gx", "gy"), None, None),
        P(("gx", "gy"), None, None),
        P(("gx", "gy"), None, None),
        P(("gx", "gy")),
        P(("gx", "gy")),
        P(),
        P(),
    )
    out_specs = (P(None, "gx", None, "gy"), P("gx", "gy", None, None), P(("gx", "gy")))
    return jax.shard_map(local, mesh=mesh, in_specs=in_specs, out_specs=out_specs, check_vma=False)
```

```python
import math

import jax
import jax.numpy as jnp
import numpy as np
from jax import lax
from jax.experimental import pallas as pl
from jax.experimental.pallas import tpu as pltpu
from jax.sharding import PartitionSpec as P

BOX = 256
CAP = 20
CHUNKS = (16, 16)
BF = jnp.bfloat16
F32 = jnp.float32
I32 = jnp.int32
VMEM_BYTES = 52 * 1024 * 1024


def dft_tables(length, gx, gy):
    n = np.arange(length)
    angles = (n[:, None] * n[None, :] % length) * (2.0 * np.pi / length)
    cosine = (np.cos(angles) / math.sqrt(length)).astype(BF)
    sine = (np.sin(angles) / math.sqrt(length)).astype(BF)
    upper = np.concatenate([cosine, sine], axis=1)
    lower = np.concatenate([-sine, cosine], axis=1)
    full = np.concatenate([upper, lower], axis=0)
    third = (
        full.reshape(2 * length, 2, gy, length // gy)
        .transpose(0, 2, 1, 3)
        .reshape(2 * length, 2 * length)
    )
    second = np.concatenate([cosine, sine], axis=1)
    local_a = length // gx
    lines = np.arange(length).reshape(gx, local_a)
    starts = np.cumsum((0,) + CHUNKS)
    rows = np.concatenate(
        [lines[:, starts[j] : starts[j + 1]].reshape(-1) for j in range(len(CHUNKS))]
    )
    first = np.concatenate([cosine[rows], sine[rows]], axis=0)
    return third, second, first


def frequencies(tile_count, block_len):
    pixel = jnp.arange(tile_count * block_len, dtype=I32).reshape(tile_count, block_len)
    freq_x = pixel % BOX
    freq_y = pixel // BOX
    freq_x = jnp.where(freq_x >= BOX // 2, freq_x - BOX, freq_x).astype(F32)
    freq_y = jnp.where(freq_y >= BOX // 2, freq_y - BOX, freq_y).astype(F32)
    radius_sq = (freq_x * freq_x + freq_y * freq_y) / (BOX * BOX / 4.0)
    return (freq_x, freq_y, radius_sq)


def params(**more):
    return pltpu.CompilerParams(vmem_limit_bytes=VMEM_BYTES, **more)


def near(x):
    return pltpu.with_memory_space_constraint(x, pltpu.VMEM)


def iota(shape, dim):
    return lax.broadcasted_iota(I32, shape, dim)


def dot(a, b):
    return jnp.dot(a, b, preferred_element_type=F32)


def shifted_index(iy, k, gy, direction):
    chips = gy // 2
    return ((iy // 2 + chips + direction * (k // 2)) % chips) * 2 + (iy % 2 + k % 2) % 2


def slots_kernel(own_ref, bid_ref, sent_ref, row_ref):
    peers = sent_ref.shape[0]
    own = jnp.concatenate([own_ref[0:1, :], own_ref[1:2, :]], axis=1)
    bid = jnp.concatenate([bid_ref[0:1, :], bid_ref[1:2, :]], axis=1)
    count = own.shape[1]
    match = iota((peers, count), 0) == own
    hot = jnp.where(match, 1.0, 0.0).astype(F32)
    before = jnp.where(iota((count, count), 0) < iota((count, count), 1), 1.0, 0.0).astype(BF)
    prefix = dot(hot.astype(BF), before)
    slot = jnp.sum(hot * prefix, axis=0, keepdims=True)
    slot_i = slot.astype(I32)
    here = iota((peers, count), 0) == slot_i
    high = jnp.where(here, ((bid >> 6) + 1).astype(F32), 0.0).astype(BF)
    low = jnp.where(here, (bid & 63).astype(F32), 0.0).astype(BF)
    nt = (((1,), (1,)), ((), ()))
    hot_b = hot.astype(BF)
    high_at = lax.dot_general(hot_b, high, nt, preferred_element_type=F32)
    low_at = lax.dot_general(hot_b, low, nt, preferred_element_type=F32)
    sent_ref[...] = (high_at * 64.0 + low_at - 64.0).astype(I32)
    row_ref[...] = own * CAP + slot_i


def lookup_kernel(ids_ref, vol_ref, out_ref, tmp_ref):
    def peer(p, carry):
        at = pl.multiple_of(p * (2 * CAP), 8)
        for s in range(CAP):
            block = jnp.maximum(ids_ref[p, s], 0)
            tmp_ref[pl.ds(at + 2 * s, 2), :] = vol_ref[pl.ds(pl.multiple_of(2 * block, 2), 2), :]
        return carry

    lax.fori_loop(0, ids_ref.shape[0], peer, 0)
    out_ref[...] = tmp_ref[...].astype(BF)


def split_parts(rows_ref, tmp_ref):
    tmp_ref[...] = rows_ref[...].astype(F32)
    count = tmp_ref.shape[0] // 2
    return tmp_ref[pl.ds(0, count, stride=2), :], tmp_ref[pl.ds(1, count, stride=2), :]


def particle_kernel(
    target_ref, ret_ref, row_ref, w_ref, shift_ref, ctf_ref, out_ref, mis_ref, tmp_ref, got_ref
):
    total = ret_ref.shape[0] // 2
    tiles = w_ref.shape[0]
    unroll = 16
    tmp_ref[...] = ret_ref[...].astype(F32)

    def fetch(i, carry):
        at = pl.multiple_of(i * (2 * unroll), 8)
        for u in range(unroll):
            source = pl.multiple_of(2 * target_ref[0, i * unroll + u], 2)
            got_ref[pl.ds(at + 2 * u, 2), :] = tmp_ref[pl.ds(source, 2), :]
        return carry

    lax.fori_loop(0, 2 * tiles // unroll, fetch, 0)
    fetched = jnp.concatenate([got_ref[pl.ds(r, 2 * tiles, stride=2), :] for r in range(2)], axis=1)
    w0 = w_ref[:, 0:1]
    w1 = w_ref[:, 1:2]
    projected = w0 * fetched[:tiles] + w1 * fetched[tiles:]
    ctf = ctf_ref[...]
    ctf2 = jnp.concatenate([ctf, ctf], axis=1)
    residual = shift_ref[...] - ctf2 * projected
    mis_ref[...] = jnp.sum(residual * residual, axis=0, keepdims=True)
    both = jnp.concatenate(
        [((w0 * ctf2) * residual).astype(BF), ((w1 * ctf2) * residual).astype(BF)], axis=0
    )
    row = row_ref[...]
    step = 512
    for b in range(total // step):
        put = jnp.where(iota((step, 2 * tiles), 0) + step * b == row, 1.0, 0.0).astype(BF)
        result = dot(put, both)
        for r in range(2):
            tmp_ref[pl.ds(2 * b * step + r, step, stride=2), :] = result[:, r * 128 : (r + 1) * 128]
    out_ref[...] = tmp_ref[...].astype(BF)


def insert_lines(first_line, inc_ref, id_ref, vol_ref, table_ref, upd_ref, tmp_ref, block_ref):
    total = block_ref.shape[0]
    lines, width = vol_ref.shape
    per_line = width // 256

    @pl.when(pl.program_id(0) == 0)
    def _():
        for r, inc in enumerate(split_parts(inc_ref, tmp_ref)):
            block_ref[:, r * 128 : (r + 1) * 128] = inc.astype(BF)

    base = first_line + pl.program_id(0) * lines
    block_id = (iota((lines, total), 0) + base) * per_line
    sums = []
    for m in range(per_line):
        pick = jnp.where(block_id + m == id_ref[...], 1.0, 0.0).astype(BF)
        sums.append(dot(pick, block_ref[...]))
    update = jnp.concatenate([x[:, r * 128 : (r + 1) * 128] for r in range(2) for x in sums], axis=1)
    upd_ref[...] = update
    inserted = (vol_ref[...].astype(F32) + update).astype(BF)
    return dot(inserted, table_ref[...])


def insert_first(inc_ref, id_ref, vol_ref, table_ref, upd_ref, out_ref, tmp_ref, block_ref):
    passed = insert_lines(0, inc_ref, id_ref, vol_ref, table_ref, upd_ref, tmp_ref, block_ref)
    for d in range(out_ref.shape[0]):
        out_ref[d] = passed[:, d * 128 : (d + 1) * 128].astype(BF)


def insert_next(first_line, iy_ref, inc_ref, id_ref, vol_ref, table_ref, old_ref, upd_ref, *refs):
    outs = refs[:-3]
    tmp_ref, block_ref, pass_ref = refs[-3:]
    passed = insert_lines(first_line, inc_ref, id_ref, vol_ref, table_ref, upd_ref, tmp_ref, block_ref)
    pass_ref[...] = passed.astype(BF)
    for k, out_ref in enumerate(outs):
        dest = shifted_index(iy_ref[0], k, len(outs), 1)
        out_ref[...] = pass_ref[:, pl.ds(pl.multiple_of(dest * 128, 128), 128)]


def second_lines(x, a, count, table_ref, tmp_ref):
    length, lanes = x.shape[0], x.shape[1] // 2
    sign = jnp.where(iota((1, 2 * lanes), 1) % lanes < lanes // 2, -1.0, 1.0).astype(F32)
    t0 = pltpu.roll(x[:, :lanes].astype(F32), lanes // 2, 1)
    t1 = pltpu.roll(x[:, lanes:].astype(F32), lanes // 2, 1)
    turned = (jnp.concatenate([t0, t1], axis=1) * sign).astype(BF)
    y = dot(table_ref[...], jnp.concatenate([x, turned], axis=0))
    tmp_ref[pl.ds(a, length, stride=count), :] = y[:, :lanes]
    tmp_ref[pl.ds(a + 1, length, stride=count), :] = y[:, lanes:]


def second_first(in_ref, table_ref, out_ref, tmp_ref):
    peers, count, rows, lanes = in_ref.shape
    length = peers * rows
    for a in range(0, count, 2):
        x = jnp.concatenate([in_ref[:, a + i].reshape(length, lanes) for i in range(2)], axis=1)
        second_lines(x, a, count, table_ref, tmp_ref)
    out_ref[...] = tmp_ref[...].astype(BF)


def second_next(iy_ref, *refs):
    ins = refs[:-4]
    table_ref, out_ref, tmp_ref, x_ref = refs[-4:]
    count, rows, lanes = ins[0].shape
    for a in range(0, count, 2):
        for k, ref in enumerate(ins):
            source = shifted_index(iy_ref[0], k, len(ins), -1)
            at = pl.ds(pl.multiple_of(source * rows, rows), rows)
            for i in range(2):
                x_ref[a // 2, at, i * lanes : (i + 1) * lanes] = ref[a + i]
    for a in range(0, count, 2):
        second_lines(x_ref[a // 2], a, count, table_ref, tmp_ref)
    out_ref[...] = tmp_ref[...].astype(BF)


def turn_rows(ref, b):
    x = ref[:, b]
    return x.reshape(x.shape[0] * x.shape[1], x.shape[2]).astype(F32).T


def turn_kernel(in_ref, out_ref):
    for b in range(in_ref.shape[1]):
        out_ref[b] = turn_rows(in_ref, b).astype(BF)


def first_kernel(*refs):
    *early_refs, late_ref, table_ref, out_ref = refs
    group = out_ref.shape[0]
    half = out_ref.shape[2]
    rows = []
    for b in range(group):
        late = turn_rows(late_ref, b).astype(BF)
        x = jnp.concatenate([ref[b] for ref in early_refs] + [late], axis=1)
        rows.append(jnp.concatenate([x, jnp.concatenate([-x[half:], x[:half]], axis=0)], axis=1))
    y = dot(jnp.concatenate(rows, axis=0), table_ref[...])
    for b in range(group):
        for s in range(2):
            at = (2 * b + s) * half
            out_ref[b, s] = y[at : at + half].astype(BF)


def local(volume, spectra, weights, owners, block_ids, pose_ids, class_ids, pose_shift, defocus):
    gx = lax.axis_size("gx")
    gy = lax.axis_size("gy")
    peers = gx * gy
    local_a, local_b, _, length = volume.shape
    tiles = spectra.shape[1]
    block_len = spectra.shape[3]
    lines = local_a * local_b
    total = peers * CAP
    rows = 2 * total
    refs = 2 * tiles
    third, second, first = dft_tables(length, gx, gy)
    whole = pl.BlockSpec(memory_space=pltpu.VMEM)

    own = owners.transpose(0, 2, 1).reshape(2, tiles)
    bid = block_ids.transpose(0, 2, 1).reshape(2, tiles)
    sent, row = pl.pallas_call(
        slots_kernel,
        out_shape=(
            jax.ShapeDtypeStruct((peers, 128), I32),
            jax.ShapeDtypeStruct((1, refs), I32),
        ),
        in_specs=[whole] * 2,
        out_specs=(whole,) * 2,
        compiler_params=params(),
        name="slots",
    )(own, bid)
    got = lax.all_to_all(
        sent.reshape(peers, 1, 128), ("gx", "gy"), split_axis=0, concat_axis=0, tiled=True
    ).reshape(peers, 128)

    scalars = pl.BlockSpec(memory_space=pltpu.SMEM)
    vol = volume.reshape(lines, 2 * length)
    per_line = length // block_len
    vol_rows = (
        volume.astype(F32)
        .reshape(lines, 2, per_line, block_len)
        .transpose(0, 2, 1, 3)
        .reshape(lines * per_line * 2, block_len)
    )
    looked = pl.pallas_call(
        lookup_kernel,
        out_shape=jax.ShapeDtypeStruct((rows, block_len), BF),
        in_specs=[scalars, whole],
        out_specs=whole,
        scratch_shapes=[pltpu.VMEM((rows, block_len), F32)],
        compiler_params=params(),
        name="lookup",
    )(got, vol_rows)
    returned = lax.all_to_all(
        looked.reshape(peers, 2 * CAP, block_len), ("gx", "gy"), split_axis=0, concat_axis=0, tiled=True
    ).reshape(rows, block_len)

    class_match = class_ids[:, None] == jnp.arange(defocus.shape[0], dtype=I32)[None, :]
    defocus_part = jnp.sum(jnp.where(class_match, defocus[None, :], 0.0), axis=1)
    pose_match = pose_ids[:, None, None] == jnp.arange(pose_shift.shape[0], dtype=I32)[None, :, None]
    shift_xy = jnp.sum(jnp.where(pose_match, pose_shift[None, :, :], 0.0), axis=1)
    freq_x, freq_y, radius_sq = frequencies(tiles, block_len)
    phase = -2.0 * math.pi / BOX * (freq_x * shift_xy[0, 0] + freq_y * shift_xy[0, 1])
    cosine = jnp.cos(phase)
    sine = jnp.sin(phase)
    spec_re = spectra[0, :, 0, :].astype(F32)
    spec_im = spectra[0, :, 1, :].astype(F32)
    shifted = jnp.concatenate([spec_re * cosine - spec_im * sine, spec_re * sine + spec_im * cosine], axis=1)
    ctf = -jnp.sin(defocus_part[0] * radius_sq + 0.1)

    ids = got[:, :CAP].reshape(1, total)
    weight = weights.reshape(tiles, 2)
    returned, ids, weight, shifted, ctf = lax.optimization_barrier((returned, ids, weight, shifted, ctf))

    outgoing, squares = pl.pallas_call(
        particle_kernel,
        out_shape=(
            jax.ShapeDtypeStruct((rows, block_len), BF),
            jax.ShapeDtypeStruct((1, 2 * block_len), F32),
        ),
        in_specs=[scalars] + [whole] * 5,
        out_specs=(whole,) * 2,
        scratch_shapes=[pltpu.VMEM((rows, block_len), F32), pltpu.VMEM((2 * refs, block_len), F32)],
        compiler_params=params(),
        name="particle",
    )(row, near(returned), row, weight, shifted, ctf)
    incoming = lax.all_to_all(
        outgoing.reshape(peers, 2 * CAP, block_len), ("gx", "gy"), split_axis=0, concat_axis=0, tiled=True
    ).reshape(rows, block_len)
    misfit = (jnp.sum(squares) / (2.0 * tiles * block_len)).reshape(1)

    iy = lax.axis_index("gy").astype(I32).reshape(1)
    step = 256
    insert_scratch = [pltpu.VMEM((rows, block_len), F32), pltpu.VMEM((total, 2 * block_len), BF)]
    update_shape = jax.ShapeDtypeStruct((lines, 2 * length), F32)

    def second_shapes(count):
        return {
            "out_shape": jax.ShapeDtypeStruct((length * count, 128), BF),
            "out_specs": whole,
            "compiler_params": params(),
        }

    def cross(x, count):
        x = x.reshape(gx, (length // gx) * count, 128)
        return lax.all_to_all(x, "gx", split_axis=0, concat_axis=0, tiled=True).reshape(
            gx, length // gx, count, 128
        )

    crossed = []
    before = None
    start = 0
    for j, count in enumerate(CHUNKS):
        chunk_lines = count * local_b
        steps = chunk_lines // step
        skip = start * local_b // step
        block = pl.BlockSpec((step, 2 * length), lambda i, skip=skip: (i + skip, 0))
        if j == 0:
            update, out = pl.pallas_call(
                insert_first,
                grid=(steps,),
                out_shape=(update_shape, jax.ShapeDtypeStruct((gy, chunk_lines, 128), BF)),
                in_specs=[whole] * 2 + [block, whole],
                out_specs=(block, pl.BlockSpec((gy, step, 128), lambda i: (0, i, 0))),
                scratch_shapes=insert_scratch,
                compiler_params=params(dimension_semantics=("arbitrary",)),
                name="insert0",
            )(near(incoming), ids, vol, third)
            arrived = lax.all_to_all(out, "gy", split_axis=0, concat_axis=0, tiled=True)
        else:
            update, *pieces = pl.pallas_call(
                lambda *r, first_line=start * local_b: insert_next(first_line, *r),
                grid=(steps,),
                out_shape=(update_shape,) + (jax.ShapeDtypeStruct((chunk_lines, 128), BF),) * gy,
                in_specs=[scalars] + [whole] * 2 + [block, whole, pl.BlockSpec(memory_space=pl.ANY)],
                out_specs=(block,) + (pl.BlockSpec((step, 128), lambda i: (i, 0)),) * gy,
                scratch_shapes=insert_scratch + [pltpu.VMEM((step, 2 * length), BF)],
                input_output_aliases={5: 0},
                compiler_params=params(dimension_semantics=("arbitrary",)),
                name=f"insert{j}",
            )(iy, incoming, ids, vol, third, update)
            before, pieces = lax.optimization_barrier((before, pieces))
            arrived = [pieces[0]]
            for k in range(1, gy):
                pairs = [(i, shifted_index(i, k, gy, 1)) for i in range(gy)]
                arrived.append(lax.ppermute(pieces[k], "gy", pairs))
        if before is not None:
            crossed.append((before, start - CHUNKS[j - 1], CHUNKS[j - 1]))
        before = arrived
        start += count
    crossed.append((before, start - CHUNKS[-1], CHUNKS[-1]))

    for j, (arrived, start, count) in enumerate(crossed):
        tmp = pltpu.VMEM((length * count, 128), F32)
        if j == 0:
            done = pl.pallas_call(
                second_first,
                in_specs=[whole] * 2,
                scratch_shapes=[tmp],
                name="second0",
                **second_shapes(count),
            )(near(arrived.reshape(gy, count, local_b, 128)), second)
        else:
            done = pl.pallas_call(
                second_next,
                in_specs=[scalars] + [whole] * (gy + 1),
                scratch_shapes=[tmp, pltpu.VMEM((count // 2, length, 256), BF)],
                name=f"second{j}",
                **second_shapes(count),
            )(iy, *[x.reshape(count, local_b, 128) for x in arrived], second)
        crossed[j] = cross(done, count)

    out_b = length // gx
    out_c = length // gy
    group = 8

    def rows_spec(count):
        return pl.BlockSpec((gx, group, count, 128), lambda i: (0, i, 0, 0))

    def turned_spec(count):
        return pl.BlockSpec((group, 128, gx * count), lambda i: (i, 0, 0))

    turned = [
        pl.pallas_call(
            turn_kernel,
            grid=(out_b // group,),
            out_shape=jax.ShapeDtypeStruct((out_b, 128, gx * count), BF),
            in_specs=[rows_spec(count)],
            out_specs=turned_spec(count),
            compiler_params=params(dimension_semantics=("arbitrary",)),
            name=f"turn{j}",
        )(crossed[j])
        for j, count in enumerate(CHUNKS[:-1])
    ]
    real_map = pl.pallas_call(
        first_kernel,
        grid=(out_b // group,),
        out_shape=jax.ShapeDtypeStruct((out_b, 2, out_c, length), BF),
        in_specs=[turned_spec(count) for count in CHUNKS[:-1]] + [rows_spec(CHUNKS[-1]), whole],
        out_specs=pl.BlockSpec((group, 2, out_c, length), lambda i: (i, 0, 0, 0)),
        compiler_params=params(dimension_semantics=("arbitrary",)),
        name="first",
    )(*turned, crossed[-1], first)
    update = update.reshape(local_a, local_b, 2, length)
    return (real_map.transpose(3, 0, 1, 2), update, misfit)


def solution(mesh):
    in_specs = (
        P("gx", "gy", None, None),
        P(("gx", "gy"), None, None, None),
        P(("gx", "gy"), None, None),
        P(("gx", "gy"), None, None),
        P(("gx", "gy"), None, None),
        P(("gx", "gy")),
        P(("gx", "gy")),
        P(),
        P(),
    )
    out_specs = (P(None, "gx", None, "gy"), P("gx", "gy", None, None), P(("gx", "gy")))
    return jax.shard_map(local, mesh=mesh, in_specs=in_specs, out_specs=out_specs, check_vma=False)
```

```python
import math

import jax
import jax.numpy as jnp
import numpy as np
from jax import lax
from jax.experimental import pallas as pl
from jax.experimental.pallas import tpu as pltpu
from jax.sharding import PartitionSpec as P

BOX = 256
CAP = 20
CHUNKS = (16, 16)
BF = jnp.bfloat16
F32 = jnp.float32
I32 = jnp.int32
VMEM_BYTES = 52 * 1024 * 1024


def dft_tables(length, gx, gy):
    n = np.arange(length)
    angles = (n[:, None] * n[None, :] % length) * (2.0 * np.pi / length)
    cosine = (np.cos(angles) / math.sqrt(length)).astype(BF)
    sine = (np.sin(angles) / math.sqrt(length)).astype(BF)
    upper = np.concatenate([cosine, sine], axis=1)
    lower = np.concatenate([-sine, cosine], axis=1)
    full = np.concatenate([upper, lower], axis=0)
    third = (
        full.reshape(2 * length, 2, gy, length // gy)
        .transpose(0, 2, 1, 3)
        .reshape(2 * length, 2 * length)
    )
    second = np.concatenate([cosine, sine], axis=1)
    local_a = length // gx
    lines = np.arange(length).reshape(gx, local_a)
    starts = np.cumsum((0,) + CHUNKS)
    rows = np.concatenate(
        [lines[:, starts[j] : starts[j + 1]].reshape(-1) for j in range(len(CHUNKS))]
    )
    first = np.concatenate([cosine[rows], sine[rows]], axis=0)
    return third, second, first


def frequencies(tile_count, block_len):
    pixel = jnp.arange(tile_count * block_len, dtype=I32).reshape(tile_count, block_len)
    freq_x = pixel % BOX
    freq_y = pixel // BOX
    freq_x = jnp.where(freq_x >= BOX // 2, freq_x - BOX, freq_x).astype(F32)
    freq_y = jnp.where(freq_y >= BOX // 2, freq_y - BOX, freq_y).astype(F32)
    radius_sq = (freq_x * freq_x + freq_y * freq_y) / (BOX * BOX / 4.0)
    return (freq_x, freq_y, radius_sq)


def params(**more):
    return pltpu.CompilerParams(vmem_limit_bytes=VMEM_BYTES, **more)


def near(x):
    return pltpu.with_memory_space_constraint(x, pltpu.VMEM)


def iota(shape, dim):
    return lax.broadcasted_iota(I32, shape, dim)


def dot(a, b):
    return jnp.dot(a, b, preferred_element_type=F32)


def shifted_index(iy, k, gy, direction):
    chips = gy // 2
    return ((iy // 2 + chips + direction * (k // 2)) % chips) * 2 + (iy % 2 + k % 2) % 2


def slots_kernel(own_ref, bid_ref, sent_ref, row_ref):
    peers = sent_ref.shape[0]
    own = jnp.concatenate([own_ref[0:1, :], own_ref[1:2, :]], axis=1)
    bid = jnp.concatenate([bid_ref[0:1, :], bid_ref[1:2, :]], axis=1)
    count = own.shape[1]
    match = iota((peers, count), 0) == own
    hot = jnp.where(match, 1.0, 0.0).astype(F32)
    before = jnp.where(iota((count, count), 0) < iota((count, count), 1), 1.0, 0.0).astype(BF)
    prefix = dot(hot.astype(BF), before)
    slot = jnp.sum(hot * prefix, axis=0, keepdims=True)
    slot_i = slot.astype(I32)
    here = iota((peers, count), 0) == slot_i
    high = jnp.where(here, ((bid >> 6) + 1).astype(F32), 0.0).astype(BF)
    low = jnp.where(here, (bid & 63).astype(F32), 0.0).astype(BF)
    nt = (((1,), (1,)), ((), ()))
    hot_b = hot.astype(BF)
    high_at = lax.dot_general(hot_b, high, nt, preferred_element_type=F32)
    low_at = lax.dot_general(hot_b, low, nt, preferred_element_type=F32)
    sent_ref[...] = (high_at * 64.0 + low_at - 64.0).astype(I32)
    row_ref[...] = own * CAP + slot_i


def lookup_kernel(ids_ref, vol_ref, out_ref, tmp_ref):
    unroll = 4

    def peers(i, carry):
        at = pl.multiple_of(i * (2 * CAP * unroll), 8)
        for j in range(unroll):
            for s in range(CAP):
                block = jnp.maximum(ids_ref[i * unroll + j, s], 0)
                row = vol_ref[pl.ds(pl.multiple_of(2 * block, 2), 2), :]
                tmp_ref[pl.ds(at + 2 * (CAP * j + s), 2), :] = row
        return carry

    lax.fori_loop(0, ids_ref.shape[0] // unroll, peers, 0)
    out_ref[...] = tmp_ref[...].astype(BF)


def split_parts(rows_ref, tmp_ref):
    tmp_ref[...] = rows_ref[...].astype(F32)
    count = tmp_ref.shape[0] // 2
    return tmp_ref[pl.ds(0, count, stride=2), :], tmp_ref[pl.ds(1, count, stride=2), :]


def particle_kernel(
    target_ref, ret_ref, row_ref, w_ref, shift_ref, ctf_ref, out_ref, mis_ref, tmp_ref, got_ref
):
    total = ret_ref.shape[0] // 2
    tiles = w_ref.shape[0]
    unroll = 16
    tmp_ref[...] = ret_ref[...].astype(F32)

    def fetch(i, carry):
        at = pl.multiple_of(i * (2 * unroll), 8)
        for u in range(unroll):
            source = pl.multiple_of(2 * target_ref[0, i * unroll + u], 2)
            got_ref[pl.ds(at + 2 * u, 2), :] = tmp_ref[pl.ds(source, 2), :]
        return carry

    lax.fori_loop(0, 2 * tiles // unroll, fetch, 0)
    fetched = jnp.concatenate([got_ref[pl.ds(r, 2 * tiles, stride=2), :] for r in range(2)], axis=1)
    w0 = w_ref[:, 0:1]
    w1 = w_ref[:, 1:2]
    projected = w0 * fetched[:tiles] + w1 * fetched[tiles:]
    ctf = ctf_ref[...]
    ctf2 = jnp.concatenate([ctf, ctf], axis=1)
    residual = shift_ref[...] - ctf2 * projected
    mis_ref[...] = jnp.sum(residual * residual, axis=0, keepdims=True)
    both = jnp.concatenate(
        [((w0 * ctf2) * residual).astype(BF), ((w1 * ctf2) * residual).astype(BF)], axis=0
    )
    row = row_ref[...]
    step = 512
    for b in range(total // step):
        put = jnp.where(iota((step, 2 * tiles), 0) + step * b == row, 1.0, 0.0).astype(BF)
        result = dot(put, both)
        for r in range(2):
            tmp_ref[pl.ds(2 * b * step + r, step, stride=2), :] = result[:, r * 128 : (r + 1) * 128]
    out_ref[...] = tmp_ref[...].astype(BF)


def insert_lines(first_line, inc_ref, id_ref, vol_ref, table_ref, upd_ref, tmp_ref, block_ref):
    total = block_ref.shape[0]
    lines, width = vol_ref.shape
    per_line = width // 256

    @pl.when(pl.program_id(0) == 0)
    def _():
        for r, inc in enumerate(split_parts(inc_ref, tmp_ref)):
            block_ref[:, r * 128 : (r + 1) * 128] = inc.astype(BF)

    base = first_line + pl.program_id(0) * lines
    block_id = (iota((lines, total), 0) + base) * per_line
    sums = []
    for m in range(per_line):
        pick = jnp.where(block_id + m == id_ref[...], 1.0, 0.0).astype(BF)
        sums.append(dot(pick, block_ref[...]))
    update = jnp.concatenate([x[:, r * 128 : (r + 1) * 128] for r in range(2) for x in sums], axis=1)
    upd_ref[...] = update
    inserted = (vol_ref[...].astype(F32) + update).astype(BF)
    return dot(inserted, table_ref[...])


def insert_first(inc_ref, id_ref, vol_ref, table_ref, upd_ref, out_ref, tmp_ref, block_ref):
    passed = insert_lines(0, inc_ref, id_ref, vol_ref, table_ref, upd_ref, tmp_ref, block_ref)
    for d in range(out_ref.shape[0]):
        out_ref[d] = passed[:, d * 128 : (d + 1) * 128].astype(BF)


def insert_next(first_line, iy_ref, inc_ref, id_ref, vol_ref, table_ref, old_ref, upd_ref, *refs):
    outs = refs[:-3]
    tmp_ref, block_ref, pass_ref = refs[-3:]
    passed = insert_lines(first_line, inc_ref, id_ref, vol_ref, table_ref, upd_ref, tmp_ref, block_ref)
    pass_ref[...] = passed.astype(BF)
    for k, out_ref in enumerate(outs):
        dest = shifted_index(iy_ref[0], k, len(outs), 1)
        out_ref[...] = pass_ref[:, pl.ds(pl.multiple_of(dest * 128, 128), 128)]


def second_lines(x, a, count, table_ref, tmp_ref):
    length, lanes = x.shape[0], x.shape[1] // 2
    sign = jnp.where(iota((1, 2 * lanes), 1) % lanes < lanes // 2, -1.0, 1.0).astype(F32)
    t0 = pltpu.roll(x[:, :lanes].astype(F32), lanes // 2, 1)
    t1 = pltpu.roll(x[:, lanes:].astype(F32), lanes // 2, 1)
    turned = (jnp.concatenate([t0, t1], axis=1) * sign).astype(BF)
    y = dot(table_ref[...], jnp.concatenate([x, turned], axis=0))
    tmp_ref[pl.ds(a, length, stride=count), :] = y[:, :lanes]
    tmp_ref[pl.ds(a + 1, length, stride=count), :] = y[:, lanes:]


def second_first(in_ref, table_ref, out_ref, tmp_ref):
    peers, count, rows, lanes = in_ref.shape
    length = peers * rows
    for a in range(0, count, 2):
        x = jnp.concatenate([in_ref[:, a + i].reshape(length, lanes) for i in range(2)], axis=1)
        second_lines(x, a, count, table_ref, tmp_ref)
    out_ref[...] = tmp_ref[...].astype(BF)


def second_next(iy_ref, *refs):
    ins = refs[:-4]
    table_ref, out_ref, tmp_ref, x_ref = refs[-4:]
    count, rows, lanes = ins[0].shape
    for a in range(0, count, 2):
        for k, ref in enumerate(ins):
            source = shifted_index(iy_ref[0], k, len(ins), -1)
            at = pl.ds(pl.multiple_of(source * rows, rows), rows)
            for i in range(2):
                x_ref[a // 2, at, i * lanes : (i + 1) * lanes] = ref[a + i]
    for a in range(0, count, 2):
        second_lines(x_ref[a // 2], a, count, table_ref, tmp_ref)
    out_ref[...] = tmp_ref[...].astype(BF)


def turn_rows(ref, b):
    x = ref[:, b]
    return x.reshape(x.shape[0] * x.shape[1], x.shape[2]).astype(F32).T


def turn_kernel(in_ref, out_ref):
    for b in range(in_ref.shape[1]):
        out_ref[b] = turn_rows(in_ref, b).astype(BF)


def first_kernel(*refs):
    *early_refs, late_ref, table_ref, out_ref = refs
    group = out_ref.shape[0]
    half = out_ref.shape[2]
    rows = []
    for b in range(group):
        late = turn_rows(late_ref, b).astype(BF)
        x = jnp.concatenate([ref[b] for ref in early_refs] + [late], axis=1)
        rows.append(jnp.concatenate([x, jnp.concatenate([-x[half:], x[:half]], axis=0)], axis=1))
    y = dot(jnp.concatenate(rows, axis=0), table_ref[...])
    for b in range(group):
        for s in range(2):
            at = (2 * b + s) * half
            out_ref[b, s] = y[at : at + half].astype(BF)


def local(volume, spectra, weights, owners, block_ids, pose_ids, class_ids, pose_shift, defocus):
    gx = lax.axis_size("gx")
    gy = lax.axis_size("gy")
    peers = gx * gy
    local_a, local_b, _, length = volume.shape
    tiles = spectra.shape[1]
    block_len = spectra.shape[3]
    lines = local_a * local_b
    total = peers * CAP
    rows = 2 * total
    refs = 2 * tiles
    third, second, first = dft_tables(length, gx, gy)
    whole = pl.BlockSpec(memory_space=pltpu.VMEM)

    own = owners.transpose(0, 2, 1).reshape(2, tiles)
    bid = block_ids.transpose(0, 2, 1).reshape(2, tiles)
    sent, row = pl.pallas_call(
        slots_kernel,
        out_shape=(
            jax.ShapeDtypeStruct((peers, 128), I32),
            jax.ShapeDtypeStruct((1, refs), I32),
        ),
        in_specs=[whole] * 2,
        out_specs=(whole,) * 2,
        compiler_params=params(),
        name="slots",
    )(*[pltpu.with_memory_space_constraint(x, pltpu.HBM) for x in (own, bid)])
    got = lax.all_to_all(
        sent.reshape(peers, 1, 128), ("gx", "gy"), split_axis=0, concat_axis=0, tiled=True
    ).reshape(peers, 128)

    scalars = pl.BlockSpec(memory_space=pltpu.SMEM)
    vol = volume.reshape(lines, 2 * length)
    per_line = length // block_len
    vol_rows = (
        volume.astype(F32)
        .reshape(lines, 2, per_line, block_len)
        .transpose(0, 2, 1, 3)
        .reshape(lines * per_line * 2, block_len)
    )
    looked = pl.pallas_call(
        lookup_kernel,
        out_shape=jax.ShapeDtypeStruct((rows, block_len), BF),
        in_specs=[scalars, whole],
        out_specs=whole,
        scratch_shapes=[pltpu.VMEM((rows, block_len), F32)],
        compiler_params=params(),
        name="lookup",
    )(got, vol_rows)
    returned = lax.all_to_all(
        looked.reshape(peers, 2 * CAP, block_len), ("gx", "gy"), split_axis=0, concat_axis=0, tiled=True
    ).reshape(rows, block_len)

    class_match = class_ids[:, None] == jnp.arange(defocus.shape[0], dtype=I32)[None, :]
    defocus_part = jnp.sum(jnp.where(class_match, defocus[None, :], 0.0), axis=1)
    pose_match = pose_ids[:, None, None] == jnp.arange(pose_shift.shape[0], dtype=I32)[None, :, None]
    shift_xy = jnp.sum(jnp.where(pose_match, pose_shift[None, :, :], 0.0), axis=1)
    freq_x, freq_y, radius_sq = frequencies(tiles, block_len)
    phase = -2.0 * math.pi / BOX * (freq_x * shift_xy[0, 0] + freq_y * shift_xy[0, 1])
    cosine = jnp.cos(phase)
    sine = jnp.sin(phase)
    spec_re = spectra[0, :, 0, :].astype(F32)
    spec_im = spectra[0, :, 1, :].astype(F32)
    shifted = jnp.concatenate([spec_re * cosine - spec_im * sine, spec_re * sine + spec_im * cosine], axis=1)
    ctf = -jnp.sin(defocus_part[0] * radius_sq + 0.1)

    ids = got[:, :CAP].reshape(1, total)
    weight = weights.reshape(tiles, 2)
    returned, ids, weight, shifted, ctf = lax.optimization_barrier((returned, ids, weight, shifted, ctf))

    outgoing, squares = pl.pallas_call(
        particle_kernel,
        out_shape=(
            jax.ShapeDtypeStruct((rows, block_len), BF),
            jax.ShapeDtypeStruct((1, 2 * block_len), F32),
        ),
        in_specs=[scalars] + [whole] * 5,
        out_specs=(whole,) * 2,
        scratch_shapes=[pltpu.VMEM((rows, block_len), F32), pltpu.VMEM((2 * refs, block_len), F32)],
        compiler_params=params(),
        name="particle",
    )(row, near(returned), row, weight, shifted, ctf)
    incoming = lax.all_to_all(
        outgoing.reshape(peers, 2 * CAP, block_len), ("gx", "gy"), split_axis=0, concat_axis=0, tiled=True
    ).reshape(rows, block_len)
    misfit = (jnp.sum(squares) / (2.0 * tiles * block_len)).reshape(1)

    iy = lax.axis_index("gy").astype(I32).reshape(1)
    step = 256
    insert_scratch = [pltpu.VMEM((rows, block_len), F32), pltpu.VMEM((total, 2 * block_len), BF)]
    update_shape = jax.ShapeDtypeStruct((lines, 2 * length), F32)

    def second_shapes(count):
        return {
            "out_shape": jax.ShapeDtypeStruct((length * count, 128), BF),
            "out_specs": whole,
            "compiler_params": params(),
        }

    def cross(x, count):
        x = x.reshape(gx, (length // gx) * count, 128)
        return lax.all_to_all(x, "gx", split_axis=0, concat_axis=0, tiled=True).reshape(
            gx, length // gx, count, 128
        )

    crossed = []
    before = None
    start = 0
    for j, count in enumerate(CHUNKS):
        chunk_lines = count * local_b
        steps = chunk_lines // step
        skip = start * local_b // step
        block = pl.BlockSpec((step, 2 * length), lambda i, skip=skip: (i + skip, 0))
        if j == 0:
            update, out = pl.pallas_call(
                insert_first,
                grid=(steps,),
                out_shape=(update_shape, jax.ShapeDtypeStruct((gy, chunk_lines, 128), BF)),
                in_specs=[whole] * 2 + [block, whole],
                out_specs=(block, pl.BlockSpec((gy, step, 128), lambda i: (0, i, 0))),
                scratch_shapes=insert_scratch,
                compiler_params=params(dimension_semantics=("arbitrary",)),
                name="insert0",
            )(near(incoming), ids, vol, third)
            arrived = lax.all_to_all(out, "gy", split_axis=0, concat_axis=0, tiled=True)
        else:
            update, *pieces = pl.pallas_call(
                lambda *r, first_line=start * local_b: insert_next(first_line, *r),
                grid=(steps,),
                out_shape=(update_shape,) + (jax.ShapeDtypeStruct((chunk_lines, 128), BF),) * gy,
                in_specs=[scalars] + [whole] * 2 + [block, whole, pl.BlockSpec(memory_space=pl.ANY)],
                out_specs=(block,) + (pl.BlockSpec((step, 128), lambda i: (i, 0)),) * gy,
                scratch_shapes=insert_scratch + [pltpu.VMEM((step, 2 * length), BF)],
                input_output_aliases={5: 0},
                compiler_params=params(dimension_semantics=("arbitrary",)),
                name=f"insert{j}",
            )(iy, incoming, ids, vol, third, update)
            before, pieces = lax.optimization_barrier((before, pieces))
            arrived = [pieces[0]]
            for k in range(1, gy):
                pairs = [(i, shifted_index(i, k, gy, 1)) for i in range(gy)]
                arrived.append(lax.ppermute(pieces[k], "gy", pairs))
        if before is not None:
            crossed.append((before, start - CHUNKS[j - 1], CHUNKS[j - 1]))
        before = arrived
        start += count
    crossed.append((before, start - CHUNKS[-1], CHUNKS[-1]))

    for j, (arrived, start, count) in enumerate(crossed):
        tmp = pltpu.VMEM((length * count, 128), F32)
        if j == 0:
            done = pl.pallas_call(
                second_first,
                in_specs=[whole] * 2,
                scratch_shapes=[tmp],
                name="second0",
                **second_shapes(count),
            )(near(arrived.reshape(gy, count, local_b, 128)), second)
        else:
            done = pl.pallas_call(
                second_next,
                in_specs=[scalars] + [whole] * (gy + 1),
                scratch_shapes=[tmp, pltpu.VMEM((count // 2, length, 256), BF)],
                name=f"second{j}",
                **second_shapes(count),
            )(iy, *[x.reshape(count, local_b, 128) for x in arrived], second)
        crossed[j] = cross(done, count)

    out_b = length // gx
    out_c = length // gy
    group = 8

    def rows_spec(count):
        return pl.BlockSpec((gx, group, count, 128), lambda i: (0, i, 0, 0))

    def turned_spec(count):
        return pl.BlockSpec((group, 128, gx * count), lambda i: (i, 0, 0))

    turned = [
        pl.pallas_call(
            turn_kernel,
            grid=(out_b // group,),
            out_shape=jax.ShapeDtypeStruct((out_b, 128, gx * count), BF),
            in_specs=[rows_spec(count)],
            out_specs=turned_spec(count),
            compiler_params=params(dimension_semantics=("arbitrary",)),
            name=f"turn{j}",
        )(crossed[j])
        for j, count in enumerate(CHUNKS[:-1])
    ]
    real_map = pl.pallas_call(
        first_kernel,
        grid=(out_b // group,),
        out_shape=jax.ShapeDtypeStruct((out_b, 2, out_c, length), BF),
        in_specs=[turned_spec(count) for count in CHUNKS[:-1]] + [rows_spec(CHUNKS[-1]), whole],
        out_specs=pl.BlockSpec((group, 2, out_c, length), lambda i: (i, 0, 0, 0)),
        compiler_params=params(dimension_semantics=("arbitrary",)),
        name="first",
    )(*turned, crossed[-1], first)
    update = update.reshape(local_a, local_b, 2, length)
    return (real_map.transpose(3, 0, 1, 2), update, misfit)


def solution(mesh):
    in_specs = (
        P("gx", "gy", None, None),
        P(("gx", "gy"), None, None, None),
        P(("gx", "gy"), None, None),
        P(("gx", "gy"), None, None),
        P(("gx", "gy"), None, None),
        P(("gx", "gy")),
        P(("gx", "gy")),
        P(),
        P(),
    )
    out_specs = (P(None, "gx", None, "gy"), P("gx", "gy", None, None), P(("gx", "gy")))
    return jax.shard_map(local, mesh=mesh, in_specs=in_specs, out_specs=out_specs, check_vma=False)
```

```python
import math

import jax
import jax.numpy as jnp
import numpy as np
from jax import lax
from jax.experimental import pallas as pl
from jax.experimental.pallas import tpu as pltpu
from jax.sharding import PartitionSpec as P

BOX = 256
CAP = 20
CHUNKS = (16, 16)
BF = jnp.bfloat16
F32 = jnp.float32
I32 = jnp.int32
VMEM_BYTES = 52 * 1024 * 1024


def dft_tables(length, gx, gy):
    n = np.arange(length)
    angles = (n[:, None] * n[None, :] % length) * (2.0 * np.pi / length)
    cosine = (np.cos(angles) / math.sqrt(length)).astype(BF)
    sine = (np.sin(angles) / math.sqrt(length)).astype(BF)
    upper = np.concatenate([cosine, sine], axis=1)
    lower = np.concatenate([-sine, cosine], axis=1)
    full = np.concatenate([upper, lower], axis=0)
    third = (
        full.reshape(2 * length, 2, gy, length // gy)
        .transpose(0, 2, 1, 3)
        .reshape(2 * length, 2 * length)
    )
    second = np.concatenate([cosine, sine], axis=1)
    local_a = length // gx
    lines = np.arange(length).reshape(gx, local_a)
    starts = np.cumsum((0,) + CHUNKS)
    rows = np.concatenate(
        [lines[:, starts[j] : starts[j + 1]].reshape(-1) for j in range(len(CHUNKS))]
    )
    first = np.concatenate([cosine[rows], sine[rows]], axis=0)
    return third, second, first


def frequencies(tile_count, block_len):
    pixel = jnp.arange(tile_count * block_len, dtype=I32).reshape(tile_count, block_len)
    freq_x = pixel % BOX
    freq_y = pixel // BOX
    freq_x = jnp.where(freq_x >= BOX // 2, freq_x - BOX, freq_x).astype(F32)
    freq_y = jnp.where(freq_y >= BOX // 2, freq_y - BOX, freq_y).astype(F32)
    radius_sq = (freq_x * freq_x + freq_y * freq_y) / (BOX * BOX / 4.0)
    return (freq_x, freq_y, radius_sq)


def params(**more):
    return pltpu.CompilerParams(vmem_limit_bytes=VMEM_BYTES, **more)


def near(x):
    return pltpu.with_memory_space_constraint(x, pltpu.VMEM)


def iota(shape, dim):
    return lax.broadcasted_iota(I32, shape, dim)


def dot(a, b):
    return jnp.dot(a, b, preferred_element_type=F32)


def shifted_index(iy, k, gy, direction):
    chips = gy // 2
    later = sorted(range(1, gy), key=lambda i: (i // 2 not in (1, chips - 1), i // 2 == 0, i % 2))
    far, core = divmod(([0] + later)[k], 2)
    return ((iy // 2 + chips + direction * far) % chips) * 2 + (iy % 2 + core) % 2


def slots_kernel(own_ref, bid_ref, sent_ref, row_ref):
    peers = sent_ref.shape[0]
    own = jnp.concatenate([own_ref[0:1, :], own_ref[1:2, :]], axis=1)
    bid = jnp.concatenate([bid_ref[0:1, :], bid_ref[1:2, :]], axis=1)
    count = own.shape[1]
    match = iota((peers, count), 0) == own
    hot = jnp.where(match, 1.0, 0.0).astype(F32)
    before = jnp.where(iota((count, count), 0) < iota((count, count), 1), 1.0, 0.0).astype(BF)
    prefix = dot(hot.astype(BF), before)
    slot = jnp.sum(hot * prefix, axis=0, keepdims=True)
    slot_i = slot.astype(I32)
    here = iota((peers, count), 0) == slot_i
    high = jnp.where(here, ((bid >> 6) + 1).astype(F32), 0.0).astype(BF)
    low = jnp.where(here, (bid & 63).astype(F32), 0.0).astype(BF)
    nt = (((1,), (1,)), ((), ()))
    hot_b = hot.astype(BF)
    high_at = lax.dot_general(hot_b, high, nt, preferred_element_type=F32)
    low_at = lax.dot_general(hot_b, low, nt, preferred_element_type=F32)
    sent_ref[...] = (high_at * 64.0 + low_at - 64.0).astype(I32)
    row_ref[...] = own * CAP + slot_i


def lookup_kernel(ids_ref, vol_ref, out_ref, tmp_ref):
    unroll = 4

    def peers(i, carry):
        at = pl.multiple_of(i * (2 * CAP * unroll), 8)
        for j in range(unroll):
            for s in range(CAP):
                block = jnp.maximum(ids_ref[i * unroll + j, s], 0)
                row = vol_ref[pl.ds(pl.multiple_of(2 * block, 2), 2), :]
                tmp_ref[pl.ds(at + 2 * (CAP * j + s), 2), :] = row
        return carry

    lax.fori_loop(0, ids_ref.shape[0] // unroll, peers, 0)
    out_ref[...] = tmp_ref[...].astype(BF)


def split_parts(rows_ref, tmp_ref):
    tmp_ref[...] = rows_ref[...].astype(F32)
    count = tmp_ref.shape[0] // 2
    return tmp_ref[pl.ds(0, count, stride=2), :], tmp_ref[pl.ds(1, count, stride=2), :]


def particle_kernel(
    target_ref, ret_ref, row_ref, w_ref, shift_ref, ctf_ref, out_ref, mis_ref, tmp_ref, got_ref
):
    total = ret_ref.shape[0] // 2
    tiles = w_ref.shape[0]
    unroll = 16
    tmp_ref[...] = ret_ref[...].astype(F32)

    def fetch(i, carry):
        at = pl.multiple_of(i * (2 * unroll), 8)
        for u in range(unroll):
            source = pl.multiple_of(2 * target_ref[0, i * unroll + u], 2)
            got_ref[pl.ds(at + 2 * u, 2), :] = tmp_ref[pl.ds(source, 2), :]
        return carry

    lax.fori_loop(0, 2 * tiles // unroll, fetch, 0)
    fetched = jnp.concatenate([got_ref[pl.ds(r, 2 * tiles, stride=2), :] for r in range(2)], axis=1)
    w0 = w_ref[:, 0:1]
    w1 = w_ref[:, 1:2]
    projected = w0 * fetched[:tiles] + w1 * fetched[tiles:]
    ctf = ctf_ref[...]
    ctf2 = jnp.concatenate([ctf, ctf], axis=1)
    residual = shift_ref[...] - ctf2 * projected
    mis_ref[...] = jnp.sum(residual * residual, axis=0, keepdims=True)
    both = jnp.concatenate(
        [((w0 * ctf2) * residual).astype(BF), ((w1 * ctf2) * residual).astype(BF)], axis=0
    )
    row = row_ref[...]
    step = 512
    for b in range(total // step):
        put = jnp.where(iota((step, 2 * tiles), 0) + step * b == row, 1.0, 0.0).astype(BF)
        result = dot(put, both)
        for r in range(2):
            tmp_ref[pl.ds(2 * b * step + r, step, stride=2), :] = result[:, r * 128 : (r + 1) * 128]
    out_ref[...] = tmp_ref[...].astype(BF)


def insert_lines(first_line, inc_ref, id_ref, vol_ref, table_ref, upd_ref, tmp_ref, block_ref):
    total = block_ref.shape[0]
    lines, width = vol_ref.shape
    per_line = width // 256

    @pl.when(pl.program_id(0) == 0)
    def _():
        for r, inc in enumerate(split_parts(inc_ref, tmp_ref)):
            block_ref[:, r * 128 : (r + 1) * 128] = inc.astype(BF)

    base = first_line + pl.program_id(0) * lines
    block_id = (iota((lines, total), 0) + base) * per_line
    sums = []
    for m in range(per_line):
        pick = jnp.where(block_id + m == id_ref[...], 1.0, 0.0).astype(BF)
        sums.append(dot(pick, block_ref[...]))
    update = jnp.concatenate([x[:, r * 128 : (r + 1) * 128] for r in range(2) for x in sums], axis=1)
    upd_ref[...] = update
    inserted = (vol_ref[...].astype(F32) + update).astype(BF)
    return dot(inserted, table_ref[...])


def insert_first(inc_ref, id_ref, vol_ref, table_ref, upd_ref, out_ref, tmp_ref, block_ref):
    passed = insert_lines(0, inc_ref, id_ref, vol_ref, table_ref, upd_ref, tmp_ref, block_ref)
    for d in range(out_ref.shape[0]):
        out_ref[d] = passed[:, d * 128 : (d + 1) * 128].astype(BF)


def insert_next(first_line, iy_ref, inc_ref, id_ref, vol_ref, table_ref, old_ref, upd_ref, *refs):
    outs = refs[:-3]
    tmp_ref, block_ref, pass_ref = refs[-3:]
    passed = insert_lines(first_line, inc_ref, id_ref, vol_ref, table_ref, upd_ref, tmp_ref, block_ref)
    pass_ref[...] = passed.astype(BF)
    for k, out_ref in enumerate(outs):
        dest = shifted_index(iy_ref[0], k, len(outs), 1)
        out_ref[...] = pass_ref[:, pl.ds(pl.multiple_of(dest * 128, 128), 128)]


def second_lines(x, a, count, table_ref, tmp_ref):
    length, lanes = x.shape[0], x.shape[1] // 2
    sign = jnp.where(iota((1, 2 * lanes), 1) % lanes < lanes // 2, -1.0, 1.0).astype(F32)
    t0 = pltpu.roll(x[:, :lanes].astype(F32), lanes // 2, 1)
    t1 = pltpu.roll(x[:, lanes:].astype(F32), lanes // 2, 1)
    turned = (jnp.concatenate([t0, t1], axis=1) * sign).astype(BF)
    y = dot(table_ref[...], jnp.concatenate([x, turned], axis=0))
    tmp_ref[pl.ds(a, length, stride=count), :] = y[:, :lanes]
    tmp_ref[pl.ds(a + 1, length, stride=count), :] = y[:, lanes:]


def second_first(in_ref, table_ref, out_ref, tmp_ref):
    peers, count, rows, lanes = in_ref.shape
    length = peers * rows
    for a in range(0, count, 2):
        x = jnp.concatenate([in_ref[:, a + i].reshape(length, lanes) for i in range(2)], axis=1)
        second_lines(x, a, count, table_ref, tmp_ref)
    out_ref[...] = tmp_ref[...].astype(BF)


def second_next(iy_ref, *refs):
    ins = refs[:-4]
    table_ref, out_ref, tmp_ref, x_ref = refs[-4:]
    count, rows, lanes = ins[0].shape
    for a in range(0, count, 2):
        for k, ref in enumerate(ins):
            source = shifted_index(iy_ref[0], k, len(ins), -1)
            at = pl.ds(pl.multiple_of(source * rows, rows), rows)
            for i in range(2):
                x_ref[a // 2, at, i * lanes : (i + 1) * lanes] = ref[a + i]
    for a in range(0, count, 2):
        second_lines(x_ref[a // 2], a, count, table_ref, tmp_ref)
    out_ref[...] = tmp_ref[...].astype(BF)


def turn_rows(ref, b):
    x = ref[:, b]
    return x.reshape(x.shape[0] * x.shape[1], x.shape[2]).astype(F32).T


def turn_kernel(in_ref, out_ref):
    for b in range(in_ref.shape[1]):
        out_ref[b] = turn_rows(in_ref, b).astype(BF)


def first_kernel(*refs):
    *early_refs, late_ref, table_ref, out_ref = refs
    group = out_ref.shape[0]
    half = out_ref.shape[2]
    rows = []
    for b in range(group):
        late = turn_rows(late_ref, b).astype(BF)
        x = jnp.concatenate([ref[b] for ref in early_refs] + [late], axis=1)
        rows.append(jnp.concatenate([x, jnp.concatenate([-x[half:], x[:half]], axis=0)], axis=1))
    y = dot(jnp.concatenate(rows, axis=0), table_ref[...])
    for b in range(group):
        for s in range(2):
            at = (2 * b + s) * half
            out_ref[b, s] = y[at : at + half].astype(BF)


def local(volume, spectra, weights, owners, block_ids, pose_ids, class_ids, pose_shift, defocus):
    gx = lax.axis_size("gx")
    gy = lax.axis_size("gy")
    peers = gx * gy
    local_a, local_b, _, length = volume.shape
    tiles = spectra.shape[1]
    block_len = spectra.shape[3]
    lines = local_a * local_b
    total = peers * CAP
    rows = 2 * total
    refs = 2 * tiles
    third, second, first = dft_tables(length, gx, gy)
    whole = pl.BlockSpec(memory_space=pltpu.VMEM)

    own = owners.transpose(0, 2, 1).reshape(2, tiles)
    bid = block_ids.transpose(0, 2, 1).reshape(2, tiles)
    sent, row = pl.pallas_call(
        slots_kernel,
        out_shape=(
            jax.ShapeDtypeStruct((peers, 128), I32),
            jax.ShapeDtypeStruct((1, refs), I32),
        ),
        in_specs=[whole] * 2,
        out_specs=(whole,) * 2,
        compiler_params=params(),
        name="slots",
    )(*[pltpu.with_memory_space_constraint(x, pltpu.HBM) for x in (own, bid)])
    got = lax.all_to_all(
        sent.reshape(peers, 1, 128), ("gx", "gy"), split_axis=0, concat_axis=0, tiled=True
    ).reshape(peers, 128)

    scalars = pl.BlockSpec(memory_space=pltpu.SMEM)
    vol = volume.reshape(lines, 2 * length)
    per_line = length // block_len
    vol_rows = (
        volume.astype(F32)
        .reshape(lines, 2, per_line, block_len)
        .transpose(0, 2, 1, 3)
        .reshape(lines * per_line * 2, block_len)
    )
    looked = pl.pallas_call(
        lookup_kernel,
        out_shape=jax.ShapeDtypeStruct((rows, block_len), BF),
        in_specs=[scalars, whole],
        out_specs=whole,
        scratch_shapes=[pltpu.VMEM((rows, block_len), F32)],
        compiler_params=params(),
        name="lookup",
    )(got, vol_rows)
    returned = lax.all_to_all(
        looked.reshape(peers, 2 * CAP, block_len), ("gx", "gy"), split_axis=0, concat_axis=0, tiled=True
    ).reshape(rows, block_len)

    class_match = class_ids[:, None] == jnp.arange(defocus.shape[0], dtype=I32)[None, :]
    defocus_part = jnp.sum(jnp.where(class_match, defocus[None, :], 0.0), axis=1)
    pose_match = pose_ids[:, None, None] == jnp.arange(pose_shift.shape[0], dtype=I32)[None, :, None]
    shift_xy = jnp.sum(jnp.where(pose_match, pose_shift[None, :, :], 0.0), axis=1)
    freq_x, freq_y, radius_sq = frequencies(tiles, block_len)
    phase = -2.0 * math.pi / BOX * (freq_x * shift_xy[0, 0] + freq_y * shift_xy[0, 1])
    cosine = jnp.cos(phase)
    sine = jnp.sin(phase)
    spec_re = spectra[0, :, 0, :].astype(F32)
    spec_im = spectra[0, :, 1, :].astype(F32)
    shifted = jnp.concatenate([spec_re * cosine - spec_im * sine, spec_re * sine + spec_im * cosine], axis=1)
    ctf = -jnp.sin(defocus_part[0] * radius_sq + 0.1)

    ids = got[:, :CAP].reshape(1, total)
    weight = weights.reshape(tiles, 2)
    returned, ids, weight, shifted, ctf = lax.optimization_barrier((returned, ids, weight, shifted, ctf))

    outgoing, squares = pl.pallas_call(
        particle_kernel,
        out_shape=(
            jax.ShapeDtypeStruct((rows, block_len), BF),
            jax.ShapeDtypeStruct((1, 2 * block_len), F32),
        ),
        in_specs=[scalars] + [whole] * 5,
        out_specs=(whole,) * 2,
        scratch_shapes=[pltpu.VMEM((rows, block_len), F32), pltpu.VMEM((2 * refs, block_len), F32)],
        compiler_params=params(),
        name="particle",
    )(row, near(returned), row, weight, shifted, ctf)
    incoming = lax.all_to_all(
        outgoing.reshape(peers, 2 * CAP, block_len), ("gx", "gy"), split_axis=0, concat_axis=0, tiled=True
    ).reshape(rows, block_len)
    misfit = (jnp.sum(squares) / (2.0 * tiles * block_len)).reshape(1)

    iy = lax.axis_index("gy").astype(I32).reshape(1)
    step = 256
    insert_scratch = [pltpu.VMEM((rows, block_len), F32), pltpu.VMEM((total, 2 * block_len), BF)]
    update_shape = jax.ShapeDtypeStruct((lines, 2 * length), F32)

    def second_shapes(count):
        return {
            "out_shape": jax.ShapeDtypeStruct((length * count, 128), BF),
            "out_specs": whole,
            "compiler_params": params(),
        }

    def cross(x, count):
        x = x.reshape(gx, (length // gx) * count, 128)
        return lax.all_to_all(x, "gx", split_axis=0, concat_axis=0, tiled=True).reshape(
            gx, length // gx, count, 128
        )

    crossed = []
    before = None
    start = 0
    for j, count in enumerate(CHUNKS):
        chunk_lines = count * local_b
        steps = chunk_lines // step
        skip = start * local_b // step
        block = pl.BlockSpec((step, 2 * length), lambda i, skip=skip: (i + skip, 0))
        if j == 0:
            update, out = pl.pallas_call(
                insert_first,
                grid=(steps,),
                out_shape=(update_shape, jax.ShapeDtypeStruct((gy, chunk_lines, 128), BF)),
                in_specs=[whole] * 2 + [block, whole],
                out_specs=(block, pl.BlockSpec((gy, step, 128), lambda i: (0, i, 0))),
                scratch_shapes=insert_scratch,
                compiler_params=params(dimension_semantics=("arbitrary",)),
                name="insert0",
            )(near(incoming), ids, vol, third)
            arrived = lax.all_to_all(out, "gy", split_axis=0, concat_axis=0, tiled=True)
        else:
            update, *pieces = pl.pallas_call(
                lambda *r, first_line=start * local_b: insert_next(first_line, *r),
                grid=(steps,),
                out_shape=(update_shape,) + (jax.ShapeDtypeStruct((chunk_lines, 128), BF),) * gy,
                in_specs=[scalars] + [whole] * 2 + [block, whole, pl.BlockSpec(memory_space=pl.ANY)],
                out_specs=(block,) + (pl.BlockSpec((step, 128), lambda i: (i, 0)),) * gy,
                scratch_shapes=insert_scratch + [pltpu.VMEM((step, 2 * length), BF)],
                input_output_aliases={5: 0},
                compiler_params=params(dimension_semantics=("arbitrary",)),
                name=f"insert{j}",
            )(iy, incoming, ids, vol, third, update)
            before, pieces = lax.optimization_barrier((before, pieces))
            arrived = [pieces[0]]
            for k in range(1, gy):
                pairs = [(i, shifted_index(i, k, gy, 1)) for i in range(gy)]
                arrived.append(lax.ppermute(pieces[k], "gy", pairs))
        if before is not None:
            crossed.append((before, start - CHUNKS[j - 1], CHUNKS[j - 1]))
        before = arrived
        start += count
    crossed.append((before, start - CHUNKS[-1], CHUNKS[-1]))

    for j, (arrived, start, count) in enumerate(crossed):
        tmp = pltpu.VMEM((length * count, 128), F32)
        if j == 0:
            done = pl.pallas_call(
                second_first,
                in_specs=[whole] * 2,
                scratch_shapes=[tmp],
                name="second0",
                **second_shapes(count),
            )(near(arrived.reshape(gy, count, local_b, 128)), second)
        else:
            done = pl.pallas_call(
                second_next,
                in_specs=[scalars] + [whole] * (gy + 1),
                scratch_shapes=[tmp, pltpu.VMEM((count // 2, length, 256), BF)],
                name=f"second{j}",
                **second_shapes(count),
            )(iy, *[x.reshape(count, local_b, 128) for x in arrived], second)
        crossed[j] = cross(done, count)

    out_b = length // gx
    out_c = length // gy
    group = 8

    def rows_spec(count):
        return pl.BlockSpec((gx, group, count, 128), lambda i: (0, i, 0, 0))

    def turned_spec(count):
        return pl.BlockSpec((group, 128, gx * count), lambda i: (i, 0, 0))

    turned = [
        pl.pallas_call(
            turn_kernel,
            grid=(out_b // group,),
            out_shape=jax.ShapeDtypeStruct((out_b, 128, gx * count), BF),
            in_specs=[rows_spec(count)],
            out_specs=turned_spec(count),
            compiler_params=params(dimension_semantics=("arbitrary",)),
            name=f"turn{j}",
        )(crossed[j])
        for j, count in enumerate(CHUNKS[:-1])
    ]
    real_map = pl.pallas_call(
        first_kernel,
        grid=(out_b // group,),
        out_shape=jax.ShapeDtypeStruct((out_b, 2, out_c, length), BF),
        in_specs=[turned_spec(count) for count in CHUNKS[:-1]] + [rows_spec(CHUNKS[-1]), whole],
        out_specs=pl.BlockSpec((group, 2, out_c, length), lambda i: (i, 0, 0, 0)),
        compiler_params=params(dimension_semantics=("arbitrary",)),
        name="first",
    )(*turned, crossed[-1], first)
    update = update.reshape(local_a, local_b, 2, length)
    return (real_map.transpose(3, 0, 1, 2), update, misfit)


def solution(mesh):
    in_specs = (
        P("gx", "gy", None, None),
        P(("gx", "gy"), None, None, None),
        P(("gx", "gy"), None, None),
        P(("gx", "gy"), None, None),
        P(("gx", "gy"), None, None),
        P(("gx", "gy")),
        P(("gx", "gy")),
        P(),
        P(),
    )
    out_specs = (P(None, "gx", None, "gy"), P("gx", "gy", None, None), P(("gx", "gy")))
    return jax.shard_map(local, mesh=mesh, in_specs=in_specs, out_specs=out_specs, check_vma=False)
```
